32 devices in a mesh: tensor: 2 (over x), dp: 4 (over y, core), context: 4 (over z).
Axes of the slice: x: 2, y: 2, z: 4, core: 2. Of those that a mesh axis runs over, the one named last changes fastest.
Arguments:
- tokens: bfloat16 [8, 2048, 1536], P('dp', 'context'), may hold values from -6 to 6
- out_grad: bfloat16 [8, 2048, 1536], P('dp', 'context'), may hold values from -6 to 6
- span_order: int32 [8], replicated, may hold values from 0 to 7, as said below
- query_weight: float32 [1536, 1536], P(('dp', 'context'), 'tensor'), may hold values from -0.15625 to 0.15625
- key_weight: float32 [1536, 768], P(('dp', 'context'), 'tensor'), may hold values from -0.15625 to 0.15625
- value_projection: float32 [1536, 768], P(('dp', 'context'), 'tensor'), may hold values from -0.15625 to 0.15625
- output_weight: float32 [1536, 1536], P('tensor', ('dp', 'context')), may hold values from -2.5 to 2.5
- gate_weight: float32 [1536, 4096], P(('dp', 'context'), 'tensor'), may hold values from -0.15625 to 0.15625
- up_weight: float32 [1536, 4096], P(('dp', 'context'), 'tensor'), may hold values from -0.15625 to 0.15625
- down_weight: float32 [4096, 1536], P('tensor', ('dp', 'context')), may hold values from -0.09375 to 0.09375
- attention_gain: float32 [1536], P(('dp', 'context')), may hold values from 0.5 to 1.5
- feedforward_gain: float32 [1536], P(('dp', 'context')), may hold values from 0.5 to 1.5
- query_weight_first: float32 [1536, 1536], P(('dp', 'context'), 'tensor'), may hold values from -48 to 48
- key_projection_first_moment: float32 [1536, 768], P(('dp', 'context'), 'tensor'), may hold values from -64 to 64
- value_projection_first_moment: float32 [1536, 768], P(('dp', 'context'), 'tensor'), may hold values from -64 to 64
- output_weight_first: float32 [1536, 1536], P('tensor', ('dp', 'context')), may hold values from -6 to 6
- gate_weight_first: float32 [1536, 4096], P(('dp', 'context'), 'tensor'), may hold values from -28 to 28
- up_weight_first: float32 [1536, 4096], P(('dp', 'context'), 'tensor'), may hold values from -28 to 28
- down_weight_first: float32 [4096, 1536], P('tensor', ('dp', 'context')), may hold values from -48 to 48
- attention_gain_first: float32 [1536], P(('dp', 'context')), may hold values from -80 to 80
- feedforward_gain_first: float32 [1536], P(('dp', 'context')), may hold values from -80 to 80
- query_weight_second: float32 [1536, 1536], P(('dp', 'context'), 'tensor'), may hold values from 180.224 to 1179.648
- key_projection_second_moment: float32 [1536, 768], P(('dp', 'context'), 'tensor'), may hold values from 360.448 to 2359.296
- value_projection_second_moment: float32 [1536, 768], P(('dp', 'context'), 'tensor'), may hold values from 360.448 to 2359.296
- output_weight_second: float32 [1536, 1536], P('tensor', ('dp', 'context')), may hold values from 0.696 to 4.64
- gate_weight_second: float32 [1536, 4096], P(('dp', 'context'), 'tensor'), may hold values from 67.584 to 442.368
- up_weight_second: float32 [1536, 4096], P(('dp', 'context'), 'tensor'), may hold values from 67.584 to 442.368
- down_weight_second: float32 [4096, 1536], P('tensor', ('dp', 'context')), may hold values from 180.224 to 1179.648
- attention_gain_second: float32 [1536], P(('dp', 'context')), may hold values from 491.52 to 3276.8
- feedforward_gain_second: float32 [1536], P(('dp', 'context')), may hold values from 491.52 to 3276.8
Outputs:
- output: float32 [8, 2048, 1536], P('dp', 'context')
- input_grad: float32 [8, 2048, 1536], P('dp', 'context')
- query_weight_gradient: float32 [1536, 1536], P(('dp', 'context'), 'tensor')
- key_weight_gradient: float32 [1536, 768], P(('dp', 'context'), 'tensor')
- value_weight_gradient: float32 [1536, 768], P(('dp', 'context'), 'tensor')
- output_weight_gradient: float32 [1536, 1536], P('tensor', ('dp', 'context'))
- gate_weight_gradient: float32 [1536, 4096], P(('dp', 'context'), 'tensor')
- up_weight_gradient: float32 [1536, 4096], P(('dp', 'context'), 'tensor')
- down_weight_gradient: float32 [4096, 1536], P('tensor', ('dp', 'context'))
- attention_gain_gradient: float32 [1536], P(('dp', 'context'))
- feedforward_gain_gradient: float32 [1536], P(('dp', 'context'))
- query_weight_updated: float32 [1536, 1536], P(('dp', 'context'), 'tensor')
- key_weight_updated: float32 [1536, 768], P(('dp', 'context'), 'tensor')
- value_weight_updated: float32 [1536, 768], P(('dp', 'context'), 'tensor')
- output_weight_updated: float32 [1536, 1536], P('tensor', ('dp', 'context'))
- gate_weight_updated: float32 [1536, 4096], P(('dp', 'context'), 'tensor')
- up_weight_updated: float32 [1536, 4096], P(('dp', 'context'), 'tensor')
- down_weight_updated: float32 [4096, 1536], P('tensor', ('dp', 'context'))
- attention_gain_updated: float32 [1536], P(('dp', 'context'))
- feedforward_gain_updated: float32 [1536], P(('dp', 'context'))
- query_weight_first_updated: float32 [1536, 1536], P(('dp', 'context'), 'tensor')
- key_weight_first_updated: float32 [1536, 768], P(('dp', 'context'), 'tensor')
- value_weight_first_updated: float32 [1536, 768], P(('dp', 'context'), 'tensor')
- output_weight_first_updated: float32 [1536, 1536], P('tensor', ('dp', 'context'))
- gate_weight_first_updated: float32 [1536, 4096], P(('dp', 'context'), 'tensor')
- up_weight_first_updated: float32 [1536, 4096], P(('dp', 'context'), 'tensor')
- down_weight_first_updated: float32 [4096, 1536], P('tensor', ('dp', 'context'))
- attention_gain_first_updated: float32 [1536], P(('dp', 'context'))
- feedforward_gain_first_updated: float32 [1536], P(('dp', 'context'))
- query_weight_second_updated: float32 [1536, 1536], P(('dp', 'context'), 'tensor')
- key_weight_second_updated: float32 [1536, 768], P(('dp', 'context'), 'tensor')
- value_weight_second_updated: float32 [1536, 768], P(('dp', 'context'), 'tensor')
- output_weight_second_updated: float32 [1536, 1536], P('tensor', ('dp', 'context'))
- gate_weight_second_updated: float32 [1536, 4096], P(('dp', 'context'), 'tensor')
- up_weight_second_updated: float32 [1536, 4096], P(('dp', 'context'), 'tensor')
- down_weight_second_updated: float32 [4096, 1536], P('tensor', ('dp', 'context'))
- attention_gain_second_updated: float32 [1536], P(('dp', 'context'))
- feedforward_gain_second_updated: float32 [1536], P(('dp', 'context'))
The draws below stay inside these ranges and needn't reach their ends.
Inputs may be any that keep to these rules, and one draw needn't show every extreme that they name: `span_order`: a permutation of 0 to 7 in which the spans of slots 2 c and 2 c + 1 add up to 7.
All inputs are finite; a program needn't handle non-finite values.
Results may differ from the reference program's by a relative error of at most 0.035.
Values may be sent and summed in bfloat16 or wider, within the bound.
No kernel may reach another device: no remote copies, remote signals or barrier semaphores. Data moves between devices by JAX's collectives and lax.ppermute only.
A program may use at most 320 MiB of HBM per device.

```python
import math
import jax
import jax.numpy as jnp
from jax import lax

MODEL_DIMENSION = 1536
QUERY_HEADS = 16
KEY_VALUE_HEADS = 8
HEAD_DIMENSION = 96
FF = 4096
SPAN = 256
SPANS = 8
SEQUENCE_LENGTH = 2048
SEQUENCES = 8
TOKEN_TOTAL = 16384


def draw_span_order(key, part):
    halfway = SPANS // 2
    leading_ids = jax.random.permutation(jax.random.fold_in(key, 3), halfway).astype(jnp.int32)
    flipped = jax.random.randint(jax.random.fold_in(key, 5), (halfway,), 0, 2, jnp.int32)
    partner = (SPANS - 1 - leading_ids).astype(jnp.int32)
    slot_even = jnp.where(flipped == 1, partner, leading_ids)
    slot_odd = jnp.where(flipped == 1, leading_ids, partner)
    return jnp.stack([slot_even, slot_odd], axis=1).reshape(SPANS).astype(jnp.int32)


def shard_levels(own_key, extent, shards, smallest, high):
    factor_of, own = 1.0, jax.random.fold_in(own_key, 6)
    for axis_at, shards_of in shards:
        steps = jnp.exp(jax.random.uniform(jax.random.fold_in(own, axis_at), (shards_of,), jnp.float32, smallest / len(shards), high / len(shards)))
        factor_of = factor_of * jnp.repeat(steps, extent[axis_at] // shards_of).reshape([-1 if axis == axis_at else 1 for axis in range(len(extent))])
    return factor_of


def scatter_about(stream_key, shape, width, most, split=(), held_as=jnp.bfloat16):
    values = width * jax.random.normal(stream_key, shape, jnp.float32)
    if split:
        values = values * shard_levels(stream_key, shape, split, -0.22, 0.18)
    return jnp.clip(values, -most, most).astype(held_as)


def setup_inputs(seed: int = 0) -> dict:
    key_of = jax.random.split(jax.random.key(seed), 31)
    return {
        "tokens": scatter_about(key_of[0], (SEQUENCES, SEQUENCE_LENGTH, MODEL_DIMENSION), 1.0, 6.0, ((0, 4), (1, 4))),
        "out_grad": scatter_about(key_of[1], (SEQUENCES, SEQUENCE_LENGTH, MODEL_DIMENSION), 1.0, 6.0, ((0, 4), (1, 4))),
        "span_order": draw_span_order(jax.random.fold_in(key_of[30], 71), 0),
        "query_weight": scatter_about(key_of[3], (MODEL_DIMENSION, QUERY_HEADS * HEAD_DIMENSION), MODEL_DIMENSION ** -0.5, 0.15625, ((0, 16), (1, 2)), jnp.float32),
        "key_weight": scatter_about(key_of[4], (MODEL_DIMENSION, KEY_VALUE_HEADS * HEAD_DIMENSION), MODEL_DIMENSION ** -0.5, 0.15625, ((0, 16), (1, 2)), jnp.float32),
        "value_projection": scatter_about(key_of[5], (MODEL_DIMENSION, KEY_VALUE_HEADS * HEAD_DIMENSION), MODEL_DIMENSION ** -0.5, 0.15625, ((0, 16), (1, 2)), jnp.float32),
        "output_weight": scatter_about(key_of[6], (QUERY_HEADS * HEAD_DIMENSION, MODEL_DIMENSION), (QUERY_HEADS * HEAD_DIMENSION * 8 // SEQUENCE_LENGTH) ** -0.5, 2.5, ((0, 2), (1, 16)), jnp.float32),
        "gate_weight": scatter_about(key_of[7], (MODEL_DIMENSION, FF), MODEL_DIMENSION ** -0.5, 0.15625, ((0, 16), (1, 2)), jnp.float32),
        "up_weight": scatter_about(key_of[8], (MODEL_DIMENSION, FF), MODEL_DIMENSION ** -0.5, 0.15625, ((0, 16), (1, 2)), jnp.float32),
        "down_weight": scatter_about(key_of[9], (FF, MODEL_DIMENSION), FF ** -0.5, 0.09375, ((0, 2), (1, 16)), jnp.float32),
        "attention_gain": jnp.clip(1.0 + 0.1 * jax.random.normal(key_of[10], (MODEL_DIMENSION,), jnp.float32), 0.5, 1.5),
        "feedforward_gain": jnp.clip(1.0 + 0.1 * jax.random.normal(key_of[11], (MODEL_DIMENSION,), jnp.float32), 0.5, 1.5),
        "query_weight_first": scatter_about(key_of[12], (MODEL_DIMENSION, QUERY_HEADS * HEAD_DIMENSION), (0.06 * (TOKEN_TOTAL * MODEL_DIMENSION / (QUERY_HEADS * HEAD_DIMENSION)) ** 0.5), 48.0, ((0, 16), (1, 2)), jnp.float32),
        "key_projection_first_moment": scatter_about(key_of[13], (MODEL_DIMENSION, KEY_VALUE_HEADS * HEAD_DIMENSION), (0.085 * (TOKEN_TOTAL * MODEL_DIMENSION / (QUERY_HEADS * HEAD_DIMENSION)) ** 0.5), 64.0, ((0, 16), (1, 2)), jnp.float32),
        "value_projection_first_moment": scatter_about(key_of[14], (MODEL_DIMENSION, KEY_VALUE_HEADS * HEAD_DIMENSION), (0.085 * (TOKEN_TOTAL * MODEL_DIMENSION / (QUERY_HEADS * HEAD_DIMENSION)) ** 0.5), 64.0, ((0, 16), (1, 2)), jnp.float32),
        "output_weight_first": scatter_about(key_of[15], (QUERY_HEADS * HEAD_DIMENSION, MODEL_DIMENSION), (0.17 * (TOKEN_TOTAL / SEQUENCE_LENGTH) ** 0.5), 6.0, ((0, 2), (1, 16)), jnp.float32),
        "gate_weight_first": scatter_about(key_of[16], (MODEL_DIMENSION, FF), (0.06 * (TOKEN_TOTAL * MODEL_DIMENSION / FF) ** 0.5), 28.0, ((0, 16), (1, 2)), jnp.float32),
        "up_weight_first": scatter_about(key_of[17], (MODEL_DIMENSION, FF), (0.06 * (TOKEN_TOTAL * MODEL_DIMENSION / FF) ** 0.5), 28.0, ((0, 16), (1, 2)), jnp.float32),
        "down_weight_first": scatter_about(key_of[18], (FF, MODEL_DIMENSION), (0.06 * TOKEN_TOTAL ** 0.5), 48.0, ((0, 2), (1, 16)), jnp.float32),
        "attention_gain_first": scatter_about(key_of[19], (MODEL_DIMENSION,), (0.1 * TOKEN_TOTAL ** 0.5), 80.0, ((0, 16),), jnp.float32),
        "feedforward_gain_first": scatter_about(key_of[20], (MODEL_DIMENSION,), (0.1 * TOKEN_TOTAL ** 0.5), 80.0, ((0, 16),), jnp.float32),
        "query_weight_second": jnp.clip(jnp.exp(math.log(1179.648) - 1.8787708 * jax.random.uniform(key_of[21], (MODEL_DIMENSION, QUERY_HEADS * HEAD_DIMENSION), jnp.float32) ** shard_levels(key_of[21], (MODEL_DIMENSION, QUERY_HEADS * HEAD_DIMENSION), ((0, 16), (1, 2)), -0.2, 0.2)), 180.224, 1179.648),
        "key_projection_second_moment": jnp.clip(jnp.exp(math.log(2359.296) - 1.8787708 * jax.random.uniform(key_of[22], (MODEL_DIMENSION, KEY_VALUE_HEADS * HEAD_DIMENSION), jnp.float32) ** shard_levels(key_of[22], (MODEL_DIMENSION, KEY_VALUE_HEADS * HEAD_DIMENSION), ((0, 16), (1, 2)), -0.2, 0.2)), 360.448, 2359.296),
        "value_projection_second_moment": jnp.clip(jnp.exp(math.log(2359.296) - 1.8787708 * jax.random.uniform(key_of[23], (MODEL_DIMENSION, KEY_VALUE_HEADS * HEAD_DIMENSION), jnp.float32) ** shard_levels(key_of[23], (MODEL_DIMENSION, KEY_VALUE_HEADS * HEAD_DIMENSION), ((0, 16), (1, 2)), -0.2, 0.2)), 360.448, 2359.296),
        "output_weight_second": jnp.clip(jnp.exp(math.log(4.64) - 1.89712 * jax.random.uniform(key_of[24], (QUERY_HEADS * HEAD_DIMENSION, MODEL_DIMENSION), jnp.float32) ** shard_levels(key_of[24], (QUERY_HEADS * HEAD_DIMENSION, MODEL_DIMENSION), ((0, 2), (1, 16)), -0.2, 0.2)), 0.696, 4.64),
        "gate_weight_second": jnp.clip(jnp.exp(math.log(442.368) - 1.87877088 * jax.random.uniform(key_of[25], (MODEL_DIMENSION, FF), jnp.float32) ** shard_levels(key_of[25], (MODEL_DIMENSION, FF), ((0, 16), (1, 2)), -0.2, 0.2)), 67.584, 442.368),
        "up_weight_second": jnp.clip(jnp.exp(math.log(442.368) - 1.87877088 * jax.random.uniform(key_of[26], (MODEL_DIMENSION, FF), jnp.float32) ** shard_levels(key_of[26], (MODEL_DIMENSION, FF), ((0, 16), (1, 2)), -0.2, 0.2)), 67.584, 442.368),
        "down_weight_second": jnp.clip(jnp.exp(math.log(1179.648) - 1.8787708 * jax.random.uniform(key_of[27], (FF, MODEL_DIMENSION), jnp.float32) ** shard_levels(key_of[27], (FF, MODEL_DIMENSION), ((0, 2), (1, 16)), -0.2, 0.2)), 180.224, 1179.648),
        "attention_gain_second": jnp.clip(jnp.exp(math.log(3276.8) - 1.89712 * jax.random.uniform(key_of[28], (MODEL_DIMENSION,), jnp.float32) ** shard_levels(key_of[28], (MODEL_DIMENSION,), ((0, 16),), -0.2, 0.2)), 491.52, 3276.8),
        "feedforward_gain_second": jnp.clip(jnp.exp(math.log(3276.8) - 1.89712 * jax.random.uniform(key_of[29], (MODEL_DIMENSION,), jnp.float32) ** shard_levels(key_of[29], (MODEL_DIMENSION,), ((0, 16),), -0.2, 0.2)), 491.52, 3276.8),
    }


@jax.custom_vjp
def reduced_precision(v):
    return lax.optimization_barrier(v.astype(jnp.bfloat16)).astype(jnp.float32)

@jax.custom_vjp
def reduced_precision_backward(v):
    return v

def low_keep(v):
    return (reduced_precision(v), None)

def low_pass(kept, grad):
    return (grad,)

def back_keep(v):
    return (v, None)

def back_low(kept, grad):
    return (reduced_precision(grad),)
reduced_precision.defvjp(low_keep, low_pass)
reduced_precision_backward.defvjp(back_keep, back_low)
norm_eps = 1e-05
rope_base = 100000.0
beta_one = 0.9
beta_two = 0.95
adam_eps = 1e-08
gain_rate = 0.6
decay_rate = 0.1
step_count = 4.0

def matrix_product(operand, matrix):
    return jnp.einsum('...i,ij->...j', operand, matrix, precision=lax.Precision.HIGHEST)

def rms_scale(values, gain):
    inverse = lax.rsqrt(lax.optimization_barrier(jnp.mean(values * values, axis=-1, keepdims=True)) + norm_eps)
    return values * inverse * gain

def rotate(values, cosine, sine_part):
    halfway = values.shape[-1] // 2
    leading = values[..., :halfway]
    trailing = values[..., halfway:]
    return jnp.concatenate([leading * cosine - trailing * sine_part, trailing * cosine + leading * sine_part], axis=-1)

def block_layout(query_vectors, positions):
    batch_groups = query_vectors.shape[0]
    query_group_width = QUERY_HEADS // KEY_VALUE_HEADS
    rows_per_block = 512 if SEQUENCE_LENGTH % 512 == 0 else SEQUENCE_LENGTH
    count_of_blocks = SEQUENCE_LENGTH // rows_per_block
    query_block_list = query_vectors.reshape(batch_groups, count_of_blocks, rows_per_block, KEY_VALUE_HEADS, query_group_width, HEAD_DIMENSION).transpose(1, 0, 2, 3, 4, 5)
    position_blocks = positions.reshape(count_of_blocks, rows_per_block)
    return (query_block_list, position_blocks)

def score_maxima(stream_in, query_matrix, projected_keys, mixer_gain, cosine, sine_part, positions):
    batch_groups = stream_in.shape[0]
    first_normalized = reduced_precision(rms_scale(stream_in, mixer_gain))
    query_vectors = reduced_precision(rotate(matrix_product(first_normalized, query_matrix).reshape(batch_groups, SEQUENCE_LENGTH, QUERY_HEADS, HEAD_DIMENSION), cosine, sine_part))
    key_rows = reduced_precision(rotate(matrix_product(first_normalized, projected_keys).reshape(batch_groups, SEQUENCE_LENGTH, KEY_VALUE_HEADS, HEAD_DIMENSION), cosine, sine_part))
    query_block_list, position_blocks = block_layout(query_vectors, positions)
    score_scale = 1.0 / math.sqrt(HEAD_DIMENSION)

    def one_block(element):
        query_block, query_positions = element
        scores = jnp.einsum('bqhgd,bkhd->bhgqk', query_block, key_rows, precision=lax.Precision.HIGHEST) * score_scale
        allowed = positions[None, :] <= query_positions[:, None]
        return lax.optimization_barrier(jnp.max(jnp.where(allowed, scores, -1e+30), axis=-1, keepdims=True))
    return lax.map(one_block, (query_block_list, position_blocks))

def attend(query_vectors, key_rows, value_row_slice, positions, maxima):
    batch_groups = query_vectors.shape[0]
    query_block_list, position_blocks = block_layout(query_vectors, positions)
    score_scale = 1.0 / math.sqrt(HEAD_DIMENSION)

    @jax.checkpoint
    def one_block(element):
        query_block, query_positions, row_max = element
        scores = reduced_precision_backward(jnp.einsum('bqhgd,bkhd->bhgqk', query_block, key_rows, precision=lax.Precision.HIGHEST) * score_scale)
        allowed = positions[None, :] <= query_positions[:, None]
        masked = jnp.where(allowed, scores, -1e+30)
        weights = jnp.where(allowed, jnp.exp(masked - row_max), 0.0)
        row_total = lax.optimization_barrier(jnp.sum(weights, axis=-1, keepdims=True))
        summed = reduced_precision_backward(jnp.einsum('bhgqk,bkhd->bhgqd', reduced_precision(weights), value_row_slice, precision=lax.Precision.HIGHEST))
        return (summed / row_total).transpose(0, 3, 1, 2, 4)
    blocked = lax.map(one_block, (query_block_list, position_blocks, maxima))
    return blocked.transpose(1, 0, 2, 3, 4, 5).reshape(batch_groups, SEQUENCE_LENGTH, QUERY_HEADS * HEAD_DIMENSION)

def layer_forward(stream_in, query_matrix, projected_keys, projected_values, output_matrix, gate_matrix, up_matrix, down_matrix, mixer_gain, forward_gain, cosine, sine_part, positions, maxima):
    batch_groups = stream_in.shape[0]
    first_normalized = reduced_precision(rms_scale(stream_in, mixer_gain))
    query_raw = reduced_precision_backward(matrix_product(first_normalized, query_matrix)).reshape(batch_groups, SEQUENCE_LENGTH, QUERY_HEADS, HEAD_DIMENSION)
    query_vectors = reduced_precision(rotate(query_raw, cosine, sine_part))
    unrotated_keys = reduced_precision_backward(matrix_product(first_normalized, projected_keys)).reshape(batch_groups, SEQUENCE_LENGTH, KEY_VALUE_HEADS, HEAD_DIMENSION)
    key_rows = reduced_precision(rotate(unrotated_keys, cosine, sine_part))
    value_row_slice = reduced_precision(reduced_precision_backward(matrix_product(first_normalized, projected_values))).reshape(batch_groups, SEQUENCE_LENGTH, KEY_VALUE_HEADS, HEAD_DIMENSION)
    mixed_heads = attend(query_vectors, key_rows, value_row_slice, positions, maxima)
    stream = stream_in + reduced_precision_backward(matrix_product(reduced_precision(mixed_heads), output_matrix))
    normed_two = reduced_precision(rms_scale(stream, forward_gain))
    gate_values = reduced_precision(reduced_precision_backward(matrix_product(normed_two, gate_matrix)))
    up_values = reduced_precision(reduced_precision_backward(matrix_product(normed_two, up_matrix)))
    hidden = reduced_precision(jax.nn.silu(gate_values) * up_values)
    return stream + reduced_precision_backward(matrix_product(hidden, down_matrix))

def adamw_update(weight, gradient, moment_one, moment_two, rate_value, decay_value):
    first_new = beta_one * moment_one + (1.0 - beta_one) * gradient
    second_new = beta_two * moment_two + (1.0 - beta_two) * gradient * gradient
    corrected = first_new / (1.0 - beta_one ** step_count) / (jnp.sqrt(second_new / (1.0 - beta_two ** step_count)) + adam_eps)
    return (weight - rate_value * (corrected + decay_value * weight), first_new, second_new)

def reference(tokens, out_grad, span_order, query_weight, key_weight, value_projection, output_weight, gate_weight, up_weight, down_weight, attention_gain, feedforward_gain, query_weight_first, key_projection_first_moment, value_projection_first_moment, output_weight_first, gate_weight_first, up_weight_first, down_weight_first, attention_gain_first, feedforward_gain_first, query_weight_second, key_projection_second_moment, value_projection_second_moment, output_weight_second, gate_weight_second, up_weight_second, down_weight_second, attention_gain_second, feedforward_gain_second):
    masters = (query_weight, key_weight, value_projection, output_weight, gate_weight, up_weight, down_weight, attention_gain, feedforward_gain)
    moments_one = (query_weight_first, key_projection_first_moment, value_projection_first_moment, output_weight_first, gate_weight_first, up_weight_first, down_weight_first, attention_gain_first, feedforward_gain_first)
    moments_two = (query_weight_second, key_projection_second_moment, value_projection_second_moment, output_weight_second, gate_weight_second, up_weight_second, down_weight_second, attention_gain_second, feedforward_gain_second)
    params = tuple((weight.astype(jnp.bfloat16).astype(jnp.float32) for weight in masters))
    positions = (span_order[:, None] * SPAN + jnp.arange(SPAN, dtype=jnp.int32)[None, :]).reshape(SEQUENCE_LENGTH).astype(jnp.int32)
    frequency = rope_base ** (-(jnp.arange(HEAD_DIMENSION // 2, dtype=jnp.float32) * 2.0) / HEAD_DIMENSION)
    angles = positions.astype(jnp.float32)[:, None] * frequency[None, :]
    cosine = jnp.cos(angles)[:, None, :]
    sine_part = jnp.sin(angles)[:, None, :]
    paired = 2 if SEQUENCES % 2 == 0 and 2 * SEQUENCE_LENGTH <= 4096 else 1
    inputs = tokens.astype(jnp.float32).reshape(SEQUENCES // paired, paired, SEQUENCE_LENGTH, MODEL_DIMENSION)
    cotangents = out_grad.astype(jnp.float32).reshape(SEQUENCES // paired, paired, SEQUENCE_LENGTH, MODEL_DIMENSION)

    def one_step(totals, element):
        stream_in, cotangent = element
        maxima = score_maxima(stream_in, params[0], params[1], params[7], cosine, sine_part, positions)

        def forward(stream_value, *weights):
            return layer_forward(stream_value, *weights, cosine, sine_part, positions, maxima)
        result, pullback = jax.vjp(forward, stream_in, *params)
        gradients = pullback(cotangent)
        return (tuple((total + gradient for total, gradient in zip(totals, gradients[1:]))), (result, gradients[0]))
    zero_sums = tuple((jnp.zeros_like(weight) for weight in params))
    totals, (outputs, in_grads) = lax.scan(one_step, zero_sums, (inputs, cotangents))
    output = outputs.reshape(SEQUENCES, SEQUENCE_LENGTH, MODEL_DIMENSION)
    input_grad = in_grads.reshape(SEQUENCES, SEQUENCE_LENGTH, MODEL_DIMENSION)
    matrix_rate = 1.0 / math.sqrt(MODEL_DIMENSION)
    output_rate = 1.0 / math.sqrt(8 * QUERY_HEADS * HEAD_DIMENSION // SEQUENCE_LENGTH)
    rates = (matrix_rate,) * 3 + (output_rate,) + (matrix_rate,) * 3 + (gain_rate,) * 2
    decays = (decay_rate,) * 7 + (0.0,) * 2
    updates = [adamw_update(weight, gradient, moment_one, moment_two, rate_value, decay_value) for weight, gradient, moment_one, moment_two, rate_value, decay_value in zip(masters, totals, moments_one, moments_two, rates, decays)]
    return (output, input_grad, totals[0], totals[1], totals[2], totals[3], totals[4], totals[5], totals[6], totals[7], totals[8], updates[0][0], updates[1][0], updates[2][0], updates[3][0], updates[4][0], updates[5][0], updates[6][0], updates[7][0], updates[8][0], updates[0][1], updates[1][1], updates[2][1], updates[3][1], updates[4][1], updates[5][1], updates[6][1], updates[7][1], updates[8][1], updates[0][2], updates[1][2], updates[2][2], updates[3][2], updates[4][2], updates[5][2], updates[6][2], updates[7][2], updates[8][2])
```

```python
import functools
import math

import jax
import jax.numpy as jnp
from jax import lax
from jax.experimental import pallas as pl
from jax.experimental.pallas import tpu as pltpu
from jax.sharding import PartitionSpec as P

MODEL_DIMENSION = 1536
QUERY_HEADS = 16
KEY_VALUE_HEADS = 8
HEAD_DIMENSION = 96
FF_TILE = 512
GRAD_TILE = 1024
SMALL = pl.CostEstimate(flops=1000, bytes_accessed=1000, transcendentals=0)
LARGE = pl.CostEstimate(flops=10**12, bytes_accessed=1000, transcendentals=0)
DP, CX, TP = "dp", "context", "tensor"


norm_eps = 1e-05
rope_base = 100000.0
beta_one = 0.9
beta_two = 0.95
adam_eps = 1e-08
gain_rate = 0.6
decay_rate = 0.1
step_count = 4.0


HD = HEAD_DIMENSION
HALF = 48
LOG2E = 1.4426950408889634
f32 = jnp.float32
bf16 = jnp.bfloat16

def nn(a, b):
    return lax.dot_general(a, b, (((1,), (0,)), ((), ())), preferred_element_type=f32)

def nt(a, b):
    return lax.dot_general(a, b, (((1,), (1,)), ((), ())), preferred_element_type=f32)

def spread_heads(kv_refs, k_heads, kv_heads, rows, base):
    for s, ref in enumerate(kv_refs):
        for h in range(kv_heads):
            k_heads[h, s * rows:(s + 1) * rows, :] = ref[:, base + h * HD: base + (h + 1) * HD]

def forward_kernel(kv_heads, group, span_rows, spans, qt, *refs):
    blocks = len(refs) - 3 - 6
    kv_refs = refs[:blocks]
    out_low, out_t, log_total = refs[blocks:blocks + 3]
    k_heads, v_t, q_wide, top, total, acc = refs[blocks + 3:]
    rows = kv_refs[0].shape[0]
    kv_width = kv_heads * HD
    wide = group * span_rows
    scale = LOG2E / math.sqrt(HD)
    spread_heads(kv_refs, k_heads, kv_heads, rows, 0)
    for s, ref in enumerate(kv_refs):
        v_t[:, s * rows:(s + 1) * rows] = ref[:, kv_width:].T
    for h in range(kv_heads):
        for i in range(2):
            q_wide[h, i] = jnp.concatenate(
                [qt[(h * group + n) * HD:(h * group + n + 1) * HD, i * span_rows:(i + 1) * span_rows]
                 for n in range(group)], axis=1)
    key_at = lax.broadcasted_iota(jnp.int32, (span_rows, wide), 0)
    query_at = lax.broadcasted_iota(jnp.int32, (span_rows, wide), 1) % span_rows
    keep = key_at <= query_at
    for i in range(2):
        for h in range(kv_heads):
            scores = nn(k_heads[h, i * span_rows:(i + 1) * span_rows, :], q_wide[h, i]) * scale
            scores = jnp.where(keep, scores, -1e30)
            peak = jnp.max(scores, axis=0, keepdims=True)
            probs = jnp.exp2(scores - peak)
            top[h, i] = peak
            total[h, i] = jnp.sum(probs, axis=0, keepdims=True)
            acc[h, i] = nn(v_t[h * HD:(h + 1) * HD, i * span_rows:(i + 1) * span_rows], probs.astype(bf16))

    def visit(j, _):
        start = pl.multiple_of(j * span_rows, span_rows)
        for i in range(2):
            @pl.when(spans[2 + j] < spans[i])
            def _():
                for h in range(kv_heads):
                    scores = nn(k_heads[h, pl.ds(start, span_rows), :], q_wide[h, i]) * scale
                    before = top[h, i]
                    peak = jnp.maximum(before, jnp.max(scores, axis=0, keepdims=True))
                    fade = jnp.exp2(before - peak)
                    probs = jnp.exp2(scores - peak)
                    top[h, i] = peak
                    total[h, i] = total[h, i] * fade + jnp.sum(probs, axis=0, keepdims=True)
                    acc[h, i] = acc[h, i] * fade + nn(
                        v_t[h * HD:(h + 1) * HD, pl.ds(start, span_rows)], probs.astype(bf16))
        return 0
    lax.fori_loop(0, 2 * blocks, visit, 0)
    for i in range(2):
        cols = slice(i * span_rows, (i + 1) * span_rows)
        for h in range(kv_heads):
            sums = total[h, i]
            whole = (acc[h, i] / sums).astype(bf16)
            level = top[h, i] + jnp.log2(sums)
            for n in range(group):
                at = h * group + n
                lanes = slice(n * span_rows, (n + 1) * span_rows)
                out_t[at * HD:(at + 1) * HD, cols] = whole[:, lanes]
                log_total[at:at + 1, cols] = level[:, lanes]
    out_low[...] = out_t[...].T

def attention_forward(spans, qt, kv_blocks):
    width, rows = qt.shape
    kv_heads = kv_blocks[0].shape[1] // (2 * HD)
    heads = width // HD
    group = heads // kv_heads
    span_rows = rows // 2
    keys = rows * len(kv_blocks)
    wide = group * span_rows
    whole = lambda: pl.BlockSpec(memory_space=pltpu.VMEM)
    return pl.pallas_call(
        functools.partial(forward_kernel, kv_heads, group, span_rows),
        in_specs=[pl.BlockSpec(memory_space=pltpu.SMEM)] + [whole() for _ in range(1 + len(kv_blocks))],
        out_specs=[whole(), whole(), whole()],
        out_shape=[jax.ShapeDtypeStruct((rows, width), bf16), jax.ShapeDtypeStruct((width, rows), bf16),
                   jax.ShapeDtypeStruct((heads, rows), f32)],
        scratch_shapes=[pltpu.VMEM((kv_heads, keys, HD), bf16), pltpu.VMEM((kv_heads * HD, keys), bf16),
                        pltpu.VMEM((kv_heads, 2, HD, wide), bf16), pltpu.VMEM((kv_heads, 2, 1, wide), f32),
                        pltpu.VMEM((kv_heads, 2, 1, wide), f32), pltpu.VMEM((kv_heads, 2, HD, wide), f32)],
        compiler_params=pltpu.CompilerParams(vmem_limit_bytes=48 * 1024 * 1024),
        cost_estimate=SMALL,
        name="attention_forward",
    )(spans, qt, *kv_blocks)

def backward_kernel(kv_heads, group, span_rows, blocks, spans, qt, dot_, out_t, log_total, cos_t, sin_t, *refs):
    kv_refs = refs[:blocks]
    dq_low, kept, sent = refs[blocks:blocks + 3]
    k_heads, v_heads, k_t, q_wide, d_wide, level, inner, dq_acc, dk_acc, dv_acc = refs[blocks + 3:]
    rows = kv_refs[0].shape[0]
    kv_width = kv_heads * HD
    wide = group * span_rows
    scale = 1.0 / math.sqrt(HD)
    spread_heads(kv_refs, k_heads, kv_heads, rows, 0)
    spread_heads(kv_refs, v_heads, kv_heads, rows, kv_width)
    for s, ref in enumerate(kv_refs):
        k_t[:, s * rows:(s + 1) * rows] = ref[:, :kv_width].T
    for h in range(kv_heads):
        for i in range(2):
            cols = slice(i * span_rows, (i + 1) * span_rows)
            heads = [slice((h * group + n) * HD, (h * group + n + 1) * HD) for n in range(group)]
            q_wide[h, i] = jnp.concatenate([qt[at, cols] for at in heads], axis=1)
            d_wide[h, i] = jnp.concatenate([dot_[at, cols] for at in heads], axis=1)
            level[h, i] = jnp.concatenate([log_total[h * group + n:h * group + n + 1, cols] for n in range(group)], axis=1)
            inner[h, i] = jnp.concatenate(
                [jnp.sum(dot_[at, cols].astype(f32) * out_t[at, cols].astype(f32), axis=0, keepdims=True) for at in heads], axis=1)
    dk_acc[...] = jnp.zeros_like(dk_acc)
    dv_acc[...] = jnp.zeros_like(dv_acc)
    key_at = lax.broadcasted_iota(jnp.int32, (span_rows, wide), 0)
    query_at = lax.broadcasted_iota(jnp.int32, (span_rows, wide), 1) % span_rows
    keep = key_at <= query_at

    def pair(h, i, at, masked):
        scores = nn(k_heads[h, at, :], q_wide[h, i]) * (scale * LOG2E)
        probs = jnp.exp2(scores - level[h, i])
        if masked:
            probs = jnp.where(keep, probs, 0.0)
        dprobs = nn(v_heads[h, at, :], d_wide[h, i])
        dscores = (probs * (dprobs - inner[h, i])).astype(bf16)
        head = slice(h * HD, (h + 1) * HD)
        dv_acc[head, at] += nt(d_wide[h, i], probs.astype(bf16))
        dk_acc[head, at] += nt(q_wide[h, i], dscores)
        step = nn(k_t[head, at], dscores)
        if masked:
            dq_acc[h, i] = step
        else:
            dq_acc[h, i] += step

    for i in range(2):
        for h in range(kv_heads):
            pair(h, i, slice(i * span_rows, (i + 1) * span_rows), True)

    def visit(j, _):
        start = pl.multiple_of(j * span_rows, span_rows)
        for i in range(2):
            @pl.when(spans[2 + j] < spans[i])
            def _():
                for h in range(kv_heads):
                    pair(h, i, pl.ds(start, span_rows), False)
        return 0
    lax.fori_loop(0, 2 * blocks, visit, 0)
    for i in range(2):
        cols = slice(i * span_rows, (i + 1) * span_rows)
        cos_part, sin_part = cos_t[:, cols], sin_t[:, cols]
        parts = []
        for h in range(kv_heads):
            for n in range(group):
                grad = dq_acc[h, i, :, n * span_rows:(n + 1) * span_rows] * scale
                lead, trail = grad[:HALF], grad[HALF:]
                parts += [(lead * cos_part + trail * sin_part).astype(bf16), (trail * cos_part - lead * sin_part).astype(bf16)]
        dq_low[cols, :] = jnp.concatenate(parts, axis=0).T
    for s in range(blocks):
        cols = slice(s * rows, (s + 1) * rows)
        ref = (kept, sent)[s % 2]
        ref[s // 2, :kv_width, :] = (dk_acc[:, cols] * scale).astype(bf16)
        ref[s // 2, kv_width:, :] = dv_acc[:, cols].astype(bf16)

def attention_backward(dot_, spans, qt, out_t, log_total, cos_t, sin_t, kv_blocks):
    width, rows = qt.shape
    kv_heads = kv_blocks[0].shape[1] // (2 * HD)
    heads = width // HD
    group = heads // kv_heads
    span_rows = rows // 2
    blocks = len(kv_blocks)
    keys = rows * blocks
    wide = group * span_rows
    kv_width = kv_heads * HD
    whole = lambda: pl.BlockSpec(memory_space=pltpu.VMEM)
    return pl.pallas_call(
        functools.partial(backward_kernel, kv_heads, group, span_rows, blocks),
        in_specs=[pl.BlockSpec(memory_space=pltpu.SMEM)] + [whole() for _ in range(6 + blocks)],
        out_specs=[whole() for _ in range(3)],
        out_shape=[jax.ShapeDtypeStruct((rows, width), bf16)] + [jax.ShapeDtypeStruct((blocks // 2, 2 * kv_width, rows), bf16)] * 2,
        scratch_shapes=[pltpu.VMEM((kv_heads, keys, HD), bf16), pltpu.VMEM((kv_heads, keys, HD), bf16),
                        pltpu.VMEM((kv_width, keys), bf16),
                        pltpu.VMEM((kv_heads, 2, HD, wide), bf16), pltpu.VMEM((kv_heads, 2, HD, wide), bf16),
                        pltpu.VMEM((kv_heads, 2, 1, wide), f32), pltpu.VMEM((kv_heads, 2, 1, wide), f32),
                        pltpu.VMEM((kv_heads, 2, HD, wide), f32),
                        pltpu.VMEM((kv_width, keys), f32), pltpu.VMEM((kv_width, keys), f32)],
        compiler_params=pltpu.CompilerParams(vmem_limit_bytes=56 * 1024 * 1024),
        cost_estimate=LARGE,
        name="attention_backward",
    )(spans, qt, dot_, out_t, log_total, cos_t, sin_t, *kv_blocks)

def project_kernel(q_width, kv_width, x, gain, w, cos_t, sin_t, n1, qt, kv):
    values = x[...].astype(f32)
    inverse = lax.rsqrt(jnp.mean(values * values, axis=-1, keepdims=True) + 1e-05)
    normed = (values * inverse * gain[...]).astype(bf16)
    n1[...] = normed
    both = nn(normed, w[:, :q_width + kv_width])
    rows = both.shape[0]
    turned = both.T
    cos_part, sin_part = cos_t[...], sin_t[...]
    parts = []
    for h in range((q_width + kv_width) // HD):
        lead = turned[h * HD:h * HD + HALF]
        trail = turned[h * HD + HALF:(h + 1) * HD]
        parts += [(lead * cos_part - trail * sin_part).astype(bf16), (trail * cos_part + lead * sin_part).astype(bf16)]
    cut = q_width // HALF
    qt[...] = jnp.concatenate(parts[:cut], axis=0)
    kv[:, :kv_width] = jnp.concatenate(parts[cut:], axis=0).T
    kv[:, kv_width:] = nn(normed, w[:, q_width + kv_width:q_width + 2 * kv_width]).astype(bf16)

def project(x, gain, w, cos_t, sin_t, q_width, kv_width):
    rows, model = x.shape
    tile = 256
    return pl.pallas_call(
        functools.partial(project_kernel, q_width, kv_width),
        grid=(rows // tile,),
        in_specs=[pl.BlockSpec((tile, model), lambda r: (r, 0)),
                  pl.BlockSpec((1, model), lambda r: (0, 0)),
                  pl.BlockSpec((model, w.shape[1]), lambda r: (0, 0)),
                  pl.BlockSpec((HALF, tile), lambda r: (0, r)),
                  pl.BlockSpec((HALF, tile), lambda r: (0, r))],
        out_specs=[pl.BlockSpec((tile, model), lambda r: (r, 0)),
                   pl.BlockSpec((q_width, tile), lambda r: (0, r)),
                   pl.BlockSpec((tile, 2 * kv_width), lambda r: (r, 0))],
        out_shape=[jax.ShapeDtypeStruct((rows, model), bf16), jax.ShapeDtypeStruct((q_width, rows), bf16),
                   jax.ShapeDtypeStruct((rows, 2 * kv_width), bf16)],
        compiler_params=pltpu.CompilerParams(vmem_limit_bytes=48 * 1024 * 1024),
        cost_estimate=SMALL,
        name="project_heads",
    )(x, gain, w, cos_t, sin_t)


def rotate(values, cosine, sine_part):
    halfway = values.shape[-1] // 2
    leading = values[..., :halfway]
    trailing = values[..., halfway:]
    return jnp.concatenate(
        [leading * cosine - trailing * sine_part, trailing * cosine + leading * sine_part], axis=-1
    )


def rotate_back(values, cosine, sine_part):
    halfway = values.shape[-1] // 2
    leading = values[..., :halfway]
    trailing = values[..., halfway:]
    return jnp.concatenate(
        [leading * cosine + trailing * sine_part, trailing * cosine - leading * sine_part], axis=-1
    )


def norm_back(values, inverse, gain, upstream):
    scaled = gain * upstream
    unit_rows = values * inverse
    result = inverse * (scaled - unit_rows * jnp.mean(scaled * unit_rows, axis=-1, keepdims=True))
    return (result, jnp.sum(upstream * unit_rows, axis=0))


def contract_rows(left_side, right_side):
    return lax.dot_general(
        left_side, right_side, (((0,), (0,)), ((), ())), preferred_element_type=jnp.float32
    )


def contract_cols(left_side, right_side):
    return lax.dot_general(
        left_side, right_side, (((1,), (1,)), ((), ())), preferred_element_type=jnp.float32
    )


def adamw_update(weight, gradient, moment_one, moment_two, rate_value, decay_value):
    first_new = beta_one * moment_one + (1.0 - beta_one) * gradient
    second_new = beta_two * moment_two + (1.0 - beta_two) * gradient * gradient
    corrected = (
        first_new
        / (1.0 - beta_one**step_count)
        / (jnp.sqrt(second_new / (1.0 - beta_two**step_count)) + adam_eps)
    )
    return (weight - rate_value * (corrected + decay_value * weight), first_new, second_new)


def plain_body(
    tokens,
    out_grad,
    span_order,
    query_weight,
    key_weight,
    value_projection,
    output_weight,
    gate_weight,
    up_weight,
    down_weight,
    attention_gain,
    feedforward_gain,
    query_weight_first,
    key_projection_first_moment,
    value_projection_first_moment,
    output_weight_first,
    gate_weight_first,
    up_weight_first,
    down_weight_first,
    attention_gain_first,
    feedforward_gain_first,
    query_weight_second,
    key_projection_second_moment,
    value_projection_second_moment,
    output_weight_second,
    gate_weight_second,
    up_weight_second,
    down_weight_second,
    attention_gain_second,
    feedforward_gain_second,
):
    bf16 = jnp.bfloat16
    f32 = jnp.float32
    gathered = (
        lax.all_gather(query_weight.astype(bf16), (DP, CX), axis=0, tiled=True),
        lax.all_gather(key_weight.astype(bf16), (DP, CX), axis=0, tiled=True),
        lax.all_gather(value_projection.astype(bf16), (DP, CX), axis=0, tiled=True),
        lax.all_gather(output_weight.astype(bf16), (DP, CX), axis=1, tiled=True),
        lax.all_gather(gate_weight.astype(bf16), (DP, CX), axis=0, tiled=True),
        lax.all_gather(up_weight.astype(bf16), (DP, CX), axis=0, tiled=True),
        lax.all_gather(down_weight.astype(bf16), (DP, CX), axis=1, tiled=True),
        lax.all_gather(attention_gain.astype(bf16), (DP, CX), axis=0, tiled=True),
        lax.all_gather(feedforward_gain.astype(bf16), (DP, CX), axis=0, tiled=True),
    )
    (
        query_matrix,
        projected_keys,
        projected_values,
        output_matrix,
        gate_matrix,
        up_matrix,
        down_matrix,
        mixer_gain,
        forward_gain,
    ) = gathered
    sequence_count, sequence_rows, model_width = tokens.shape
    token_count = sequence_count * sequence_rows
    tensor_size = lax.axis_size(TP)
    own_rows = token_count // tensor_size
    span_rows = sequence_rows // 2
    span_total = span_order.shape[0]
    full_rows = span_total * span_rows
    local_heads = query_matrix.shape[1] // HEAD_DIMENSION
    kv_heads = projected_keys.shape[1] // HEAD_DIMENSION
    query_group_width = local_heads // kv_heads
    score_scale = 1.0 / math.sqrt(HEAD_DIMENSION)
    all_positions = (
        span_order[:, None] * span_rows + jnp.arange(span_rows, dtype=jnp.int32)[None, :]
    ).reshape(full_rows)
    context_index = lax.axis_index(CX)
    query_positions = lax.dynamic_slice_in_dim(
        all_positions, context_index * sequence_rows, sequence_rows
    )
    frequency = rope_base ** (-(jnp.arange(HEAD_DIMENSION // 2, dtype=f32) * 2.0) / HEAD_DIMENSION)
    angles = query_positions.astype(f32)[:, None] * frequency[None, :]
    cosine = jnp.cos(angles)[:, None, :]
    sine_part = jnp.sin(angles)[:, None, :]
    stream_in = tokens.astype(f32).reshape(token_count, model_width)
    inverse_one = lax.rsqrt(jnp.mean(stream_in * stream_in, axis=-1, keepdims=True) + norm_eps)
    mixer_scale = mixer_gain.astype(f32)
    first_normalized = (stream_in * inverse_one * mixer_scale).astype(bf16)
    query_raw = jnp.dot(first_normalized, query_matrix, preferred_element_type=f32).reshape(
        sequence_count, sequence_rows, local_heads, HEAD_DIMENSION
    )
    query_vectors = (
        rotate(query_raw, cosine, sine_part)
        .astype(bf16)
        .reshape(sequence_count, sequence_rows, kv_heads, query_group_width, HEAD_DIMENSION)
        .transpose(0, 2, 3, 1, 4)
    )
    unrotated_keys = jnp.dot(first_normalized, projected_keys, preferred_element_type=f32).reshape(
        sequence_count, sequence_rows, kv_heads, HEAD_DIMENSION
    )
    key_rows = (
        rotate(unrotated_keys, cosine, sine_part)
        .astype(bf16)
        .reshape(sequence_count, sequence_rows, kv_heads * HEAD_DIMENSION)
    )
    value_row_slice = (
        jnp.dot(first_normalized, projected_values, preferred_element_type=f32)
        .astype(bf16)
        .reshape(sequence_count, sequence_rows, kv_heads * HEAD_DIMENSION)
    )
    pieces = (
        lax.all_gather(key_rows, CX, axis=1, tiled=True),
        lax.all_gather(value_row_slice, CX, axis=1, tiled=True),
    )
    row_max = jnp.full((sequence_count, kv_heads, query_group_width, sequence_rows), -1e30, f32)
    piece_rows = pieces[0].shape[1]
    key_grid = pieces[0].reshape(sequence_count, piece_rows, kv_heads, HEAD_DIMENSION)
    value_grid = pieces[1].reshape(sequence_count, piece_rows, kv_heads, HEAD_DIMENSION)
    scores = (
        jnp.einsum("shgqd,skhd->shgqk", query_vectors, key_grid, preferred_element_type=f32)
        * score_scale
    )
    allowed = all_positions[None, :] <= query_positions[:, None]
    new_max = jnp.maximum(row_max, jnp.max(jnp.where(allowed, scores, -1e30), axis=-1))
    weights = jnp.where(allowed, jnp.exp(scores - new_max[..., None]), 0.0)
    row_total = jnp.sum(weights, axis=-1)
    summed = jnp.einsum(
        "shgqk,skhd->shgqd", weights.astype(bf16), value_grid, preferred_element_type=f32
    )
    row_max, row_total, summed = (new_max, row_total, summed)
    attention_out = summed / row_total[..., None]
    attention_low = (
        attention_out.transpose(0, 3, 1, 2, 4)
        .reshape(token_count, local_heads * HEAD_DIMENSION)
        .astype(bf16)
    )
    mixed_own = lax.psum_scatter(
        jnp.dot(attention_low, output_matrix, preferred_element_type=f32).astype(jnp.bfloat16),
        TP,
        scatter_dimension=0,
        tiled=True,
    ).astype(jnp.float32)
    tensor_index = lax.axis_index(TP)
    stream_own = (
        lax.dynamic_slice_in_dim(stream_in, tensor_index * own_rows, own_rows, 0) + mixed_own
    )
    stream_mid = lax.all_gather(
        stream_own.astype(jnp.bfloat16), TP, axis=0, tiled=True
    ).astype(stream_own.dtype)
    inverse_two = lax.rsqrt(jnp.mean(stream_mid * stream_mid, axis=-1, keepdims=True) + norm_eps)
    forward_scale = forward_gain.astype(f32)
    normed_two = (stream_mid * inverse_two * forward_scale).astype(bf16)
    gate_float = (
        jnp.dot(normed_two, gate_matrix, preferred_element_type=f32).astype(bf16).astype(f32)
    )
    up_float = jnp.dot(normed_two, up_matrix, preferred_element_type=f32).astype(bf16).astype(f32)
    sigmoid = jax.nn.sigmoid(gate_float)
    hidden = (gate_float * sigmoid * up_float).astype(bf16)
    feed_terms = jnp.dot(hidden, down_matrix, preferred_element_type=f32)
    feed_sum = lax.psum(feed_terms.astype(jnp.bfloat16), TP).astype(jnp.float32)
    output_field = (stream_mid + feed_sum).reshape(sequence_count, sequence_rows, model_width)
    upstream = out_grad.reshape(token_count, model_width)
    hidden_grad = contract_cols(upstream, down_matrix)
    down_grad = contract_rows(hidden, upstream)
    gate_grad_low = (
        hidden_grad * up_float * sigmoid * (1.0 + gate_float * (1.0 - sigmoid))
    ).astype(bf16)
    up_grad_low = (hidden_grad * gate_float * sigmoid).astype(bf16)
    gate_grad = contract_rows(normed_two, gate_grad_low)
    up_grad = contract_rows(normed_two, up_grad_low)
    normed_two_grad = lax.psum_scatter(
        (contract_cols(gate_grad_low, gate_matrix) + contract_cols(up_grad_low, up_matrix)).astype(
            jnp.bfloat16
        ),
        TP,
        scatter_dimension=0,
        tiled=True,
    ).astype(jnp.float32)
    inverse_own = lax.dynamic_slice_in_dim(inverse_two, tensor_index * own_rows, own_rows, 0)
    stream_back, forward_gain_part = norm_back(
        stream_own, inverse_own, forward_scale, normed_two_grad
    )
    stream_grad_own = (
        lax.dynamic_slice_in_dim(upstream, tensor_index * own_rows, own_rows, 0).astype(f32)
        + stream_back
    )
    stream_grad = lax.all_gather(
        stream_grad_own.astype(jnp.bfloat16), TP, axis=0, tiled=True
    ).astype(stream_grad_own.dtype)
    stream_grad_low = stream_grad.astype(bf16)
    output_grad = contract_rows(attention_low, stream_grad_low)
    attention_grad = contract_cols(stream_grad_low, output_matrix)
    head_grad = attention_grad.reshape(
        sequence_count, sequence_rows, kv_heads, query_group_width, HEAD_DIMENSION
    ).transpose(0, 2, 3, 1, 4)
    key_again, value_again = (
        lax.all_gather(key_rows, CX, axis=1, tiled=True),
        lax.all_gather(value_row_slice, CX, axis=1, tiled=True),
    )

    def sequence_back(element):
        query_seq, key_seq, value_seq, max_seq, total_seq, out_seq, grad_seq = element
        key_grid = key_seq.reshape(full_rows, kv_heads, HEAD_DIMENSION)
        value_grid = value_seq.reshape(full_rows, kv_heads, HEAD_DIMENSION)
        accum_grad = (grad_seq / total_seq[..., None]).astype(bf16)
        row_term = jnp.sum(grad_seq * out_seq, axis=-1) / total_seq
        scores = (
            jnp.einsum("hgqd,khd->hgqk", query_seq, key_grid, preferred_element_type=f32)
            * score_scale
        )
        allowed = all_positions[None, :] <= query_positions[:, None]
        weights = jnp.where(allowed, jnp.exp(scores - max_seq[..., None]), 0.0)
        value_dot = jnp.einsum("hgqd,khd->hgqk", accum_grad, value_grid, preferred_element_type=f32)
        score_grad = (weights * (value_dot - row_term[..., None])).astype(bf16)
        query_part = (
            jnp.einsum("hgqk,khd->hgqd", score_grad, key_grid, preferred_element_type=f32)
            * score_scale
        )
        key_part = (
            jnp.einsum("hgqk,hgqd->khd", score_grad, query_seq, preferred_element_type=f32)
            * score_scale
        )
        value_part = jnp.einsum(
            "hgqk,hgqd->khd", weights.astype(bf16), accum_grad, preferred_element_type=f32
        )
        return (
            query_part,
            key_part.reshape(full_rows, kv_heads * HEAD_DIMENSION),
            value_part.reshape(full_rows, kv_heads * HEAD_DIMENSION),
        )

    query_grads, key_grads, value_grads = lax.map(
        sequence_back,
        (query_vectors, key_again, value_again, row_max, row_total, attention_out, head_grad),
    )
    key_shards, value_shards = (
        lax.psum_scatter(
            key_grads.astype(jnp.bfloat16), CX, scatter_dimension=1, tiled=True
        ).astype(jnp.float32),
        lax.psum_scatter(
            value_grads.astype(jnp.bfloat16), CX, scatter_dimension=1, tiled=True
        ).astype(jnp.float32),
    )
    query_back = (
        rotate_back(
            query_grads.transpose(0, 3, 1, 2, 4).reshape(
                sequence_count, sequence_rows, local_heads, HEAD_DIMENSION
            ),
            cosine,
            sine_part,
        )
        .reshape(token_count, local_heads * HEAD_DIMENSION)
        .astype(bf16)
    )
    key_back = (
        rotate_back(
            key_shards.reshape(sequence_count, sequence_rows, kv_heads, HEAD_DIMENSION),
            cosine,
            sine_part,
        )
        .reshape(token_count, kv_heads * HEAD_DIMENSION)
        .astype(bf16)
    )
    value_back = value_shards.reshape(token_count, kv_heads * HEAD_DIMENSION).astype(bf16)
    query_wgrad = contract_rows(first_normalized, query_back)
    key_wgrad = contract_rows(first_normalized, key_back)
    value_wgrad = contract_rows(first_normalized, value_back)
    normed_one_part = (
        contract_cols(query_back, query_matrix)
        + contract_cols(key_back, projected_keys)
        + contract_cols(value_back, projected_values)
    )
    normed_one_grad, forward_gain_sum = (
        lax.psum(normed_one_part.astype(jnp.bfloat16), TP).astype(jnp.float32),
        lax.psum(forward_gain_part.astype(jnp.bfloat16), TP).astype(jnp.float32),
    )
    mixer_back, mixer_gain_part = norm_back(stream_in, inverse_one, mixer_scale, normed_one_grad)
    input_field = (stream_grad + mixer_back).reshape(sequence_count, sequence_rows, model_width)
    shards = (
        lax.psum_scatter(
            query_wgrad.astype(jnp.bfloat16), (DP, CX), scatter_dimension=0, tiled=True
        ).astype(jnp.float32),
        lax.psum_scatter(
            key_wgrad.astype(jnp.bfloat16), (DP, CX), scatter_dimension=0, tiled=True
        ).astype(jnp.float32),
        lax.psum_scatter(
            value_wgrad.astype(jnp.bfloat16), (DP, CX), scatter_dimension=0, tiled=True
        ).astype(jnp.float32),
        lax.psum_scatter(
            output_grad.astype(jnp.bfloat16), (DP, CX), scatter_dimension=1, tiled=True
        ).astype(jnp.float32),
        lax.psum_scatter(
            gate_grad.astype(jnp.bfloat16), (DP, CX), scatter_dimension=0, tiled=True
        ).astype(jnp.float32),
        lax.psum_scatter(
            up_grad.astype(jnp.bfloat16), (DP, CX), scatter_dimension=0, tiled=True
        ).astype(jnp.float32),
        lax.psum_scatter(
            down_grad.astype(jnp.bfloat16), (DP, CX), scatter_dimension=1, tiled=True
        ).astype(jnp.float32),
        lax.psum_scatter(
            mixer_gain_part.astype(jnp.bfloat16), (DP, CX), scatter_dimension=0, tiled=True
        ).astype(jnp.float32),
        lax.psum_scatter(
            forward_gain_sum.astype(jnp.bfloat16),
            (DP, CX),
            scatter_dimension=0,
            tiled=True,
        ).astype(jnp.float32),
    )
    masters = (
        query_weight,
        key_weight,
        value_projection,
        output_weight,
        gate_weight,
        up_weight,
        down_weight,
        attention_gain,
        feedforward_gain,
    )
    moments_one = (
        query_weight_first,
        key_projection_first_moment,
        value_projection_first_moment,
        output_weight_first,
        gate_weight_first,
        up_weight_first,
        down_weight_first,
        attention_gain_first,
        feedforward_gain_first,
    )
    moments_two = (
        query_weight_second,
        key_projection_second_moment,
        value_projection_second_moment,
        output_weight_second,
        gate_weight_second,
        up_weight_second,
        down_weight_second,
        attention_gain_second,
        feedforward_gain_second,
    )
    matrix_rate = 1.0 / math.sqrt(MODEL_DIMENSION)
    output_rate = 1.0 / math.sqrt(8 * QUERY_HEADS * HEAD_DIMENSION // full_rows)
    rates = (matrix_rate,) * 3 + (output_rate,) + (matrix_rate,) * 3 + (gain_rate,) * 2
    decays = (decay_rate,) * 7 + (0.0,) * 2
    updates = [
        adamw_update(weight, gradient, moment_one, moment_two, rate_value, decay_value)
        for weight, gradient, moment_one, moment_two, rate_value, decay_value in zip(
            masters, shards, moments_one, moments_two, rates, decays
        )
    ]
    return (
        output_field,
        input_field,
        shards[0],
        shards[1],
        shards[2],
        shards[3],
        shards[4],
        shards[5],
        shards[6],
        shards[7],
        shards[8],
        updates[0][0],
        updates[1][0],
        updates[2][0],
        updates[3][0],
        updates[4][0],
        updates[5][0],
        updates[6][0],
        updates[7][0],
        updates[8][0],
        updates[0][1],
        updates[1][1],
        updates[2][1],
        updates[3][1],
        updates[4][1],
        updates[5][1],
        updates[6][1],
        updates[7][1],
        updates[8][1],
        updates[0][2],
        updates[1][2],
        updates[2][2],
        updates[3][2],
        updates[4][2],
        updates[5][2],
        updates[6][2],
        updates[7][2],
        updates[8][2],
    )


def hidden_kernel(tile, normed, upstream, both_w, down_w, hidden, dboth, dnormed, acc):
    gate_up = nn(normed[...], both_w[...]).astype(bf16).astype(f32)
    gate, up = gate_up[:, :tile], gate_up[:, tile:]
    sigmoid = 1.0 / (1.0 + jnp.exp(-gate))
    silu = gate * sigmoid
    hidden[...] = (silu * up).astype(bf16)
    dhidden = nn(upstream[...], down_w[...])
    dgate = dhidden * up * sigmoid * (1.0 + gate * (1.0 - sigmoid))
    dboth_low = jnp.concatenate([dgate.astype(bf16), (dhidden * silu).astype(bf16)], axis=1)
    dboth[...] = dboth_low
    step = nt(dboth_low, both_w[...])

    @pl.when(pl.program_id(0) == 0)
    def _():
        acc[...] = step

    @pl.when(pl.program_id(0) > 0)
    def _():
        acc[...] += step

    @pl.when(pl.program_id(0) == pl.num_programs(0) - 1)
    def _():
        dnormed[...] = acc[...].astype(bf16)


def feed_forward(normed, upstream, weights, ff):
    rows, model = normed.shape
    tile = FF_TILE
    tiles = ff // tile
    whole = pl.BlockSpec((rows, model), lambda j: (0, 0))
    return pl.pallas_call(
        functools.partial(hidden_kernel, tile),
        grid=(tiles,),
        in_specs=[
            whole,
            whole,
            pl.BlockSpec((model, 2 * tile), lambda j: (0, j)),
            pl.BlockSpec((model, tile), lambda j: (0, 2 * tiles + j)),
        ],
        out_specs=[
            pl.BlockSpec((rows, tile), lambda j: (0, j)),
            pl.BlockSpec((rows, 2 * tile), lambda j: (0, j)),
            whole,
        ],
        out_shape=[
            jax.ShapeDtypeStruct((rows, ff), bf16),
            jax.ShapeDtypeStruct((rows, 2 * ff), bf16),
            jax.ShapeDtypeStruct((rows, model), bf16),
        ],
        scratch_shapes=[pltpu.VMEM((rows, model), f32)],
        compiler_params=pltpu.CompilerParams(vmem_limit_bytes=56 * 1024 * 1024),
        cost_estimate=LARGE,
        name="feed_forward",
    )(normed, upstream, weights, weights)


def mix_kernel(x, own, other, gain, w_own, w_other, stream, normed):
    total = x[...].astype(f32) + nt(own[...], w_own[...]) + nt(other[...], w_other[...])
    stream[...] = total
    inverse = lax.rsqrt(jnp.mean(total * total, axis=-1, keepdims=True) + norm_eps)
    normed[...] = (total * inverse * gain[...]).astype(bf16)


def mix_heads(x, own, other, gain, weights, first_col):
    rows, model = x.shape
    width = own.shape[1]
    tile = 256
    at = first_col // width
    row_block = lambda cols: pl.BlockSpec((tile, cols), lambda r: (r, 0))
    return pl.pallas_call(
        mix_kernel,
        grid=(rows // tile,),
        in_specs=[
            row_block(model),
            row_block(width),
            row_block(width),
            pl.BlockSpec((1, model), lambda r: (0, 0)),
            pl.BlockSpec((model, width), lambda r: (0, at)),
            pl.BlockSpec((model, width), lambda r: (0, at + 1)),
        ],
        out_specs=[row_block(model), row_block(model)],
        out_shape=[
            jax.ShapeDtypeStruct((rows, model), f32),
            jax.ShapeDtypeStruct((rows, model), bf16),
        ],
        compiler_params=pltpu.CompilerParams(vmem_limit_bytes=48 * 1024 * 1024),
        cost_estimate=SMALL,
        name="mix_heads",
    )(x, own, other, gain, weights, weights)


def stream_back_kernel(stream, upstream, own, other, gain, w, dstream, dlow, dheads):
    values = stream[...]
    inverse = lax.rsqrt(jnp.mean(values * values, axis=-1, keepdims=True) + norm_eps)
    unit = values * inverse
    scaled = gain[...] * (own[...].astype(f32) + other[...].astype(f32))
    back = inverse * (scaled - unit * jnp.mean(scaled * unit, axis=-1, keepdims=True))
    total = upstream[...].astype(f32) + back
    dstream[...] = total
    low = total.astype(bf16)
    dlow[...] = low
    dheads[...] = nn(low, w[...]).astype(bf16).T


def stream_back(other, stream, upstream, own, gain, weights, first_col, width):
    rows, model = stream.shape
    tile = 256
    at = first_col // width
    row_block = pl.BlockSpec((tile, model), lambda r: (r, 0))
    return pl.pallas_call(
        stream_back_kernel,
        grid=(rows // tile,),
        in_specs=[row_block] * 4
        + [pl.BlockSpec((1, model), lambda r: (0, 0)), pl.BlockSpec((model, width), lambda r: (0, at))],
        out_specs=[row_block, row_block, pl.BlockSpec((width, tile), lambda r: (0, r))],
        out_shape=[
            jax.ShapeDtypeStruct((rows, model), f32),
            jax.ShapeDtypeStruct((rows, model), bf16),
            jax.ShapeDtypeStruct((width, rows), bf16),
        ],
        compiler_params=pltpu.CompilerParams(vmem_limit_bytes=48 * 1024 * 1024),
        cost_estimate=LARGE,
        name="stream_back",
    )(stream, upstream, own, other, gain, weights)


def gradient_kernel(count, order, *refs):
    left, right = refs[:2 * count], refs[2 * count:3 * count]
    kept, sent = refs[3 * count:]
    total = 0.0
    for s in range(count):
        rows = jnp.concatenate([left[2 * s][...], left[2 * s + 1][...]], axis=1)
        total = total + lax.dot_general(
            rows, right[s][...], (((0,), (0,)), ((), ())), preferred_element_type=f32
        )
    low = total.astype(bf16)

    @pl.when(pl.program_id(0) == 0)
    def _():
        kept[...] = low

    @pl.when(pl.program_id(0) == 1)
    def _():
        sent[...] = low


def gradient(left, right, order, tile):
    rows, model = left[0].shape
    cols = right[0].shape[1]
    quarter = model // 4
    tiles = cols // tile
    count = len(left)
    left_specs = [
        pl.BlockSpec((rows, quarter), functools.partial(lambda p, h, c, order: (0, order[2 * h + p]), p))
        for p in range(2)
    ]
    return pl.pallas_call(
        functools.partial(gradient_kernel, count),
        grid_spec=pltpu.PrefetchScalarGridSpec(
            num_scalar_prefetch=1,
            grid=(2, tiles),
            in_specs=left_specs * count
            + [pl.BlockSpec((rows, tile), lambda h, c, order: (0, c))] * count,
            out_specs=[
                pl.BlockSpec((2 * quarter, tile), lambda h, c, order: (0, jnp.where(h == 0, c, tiles - 1))),
                pl.BlockSpec((2 * quarter, tile), lambda h, c, order: (0, jnp.where(h == 0, 0, c))),
            ],
        ),
        out_shape=[jax.ShapeDtypeStruct((2 * quarter, cols), bf16)] * 2,
        compiler_params=pltpu.CompilerParams(vmem_limit_bytes=56 * 1024 * 1024),
        cost_estimate=LARGE,
        name="gradient",
    )(order, *[each for part in left for each in (part, part)], *right)


def feed_kernel(hidden, w, out):
    out[...] = nt(hidden[...], w[...]).astype(bf16)


def feed_out(hidden, weights, first_col):
    rows, ff = hidden.shape
    model = weights.shape[0]
    tile = 512
    return pl.pallas_call(
        feed_kernel,
        grid=(model // tile,),
        in_specs=[
            pl.BlockSpec((rows, ff), lambda c: (0, 0)),
            pl.BlockSpec((tile, ff), lambda c: (c, first_col // ff)),
        ],
        out_specs=pl.BlockSpec((rows, tile), lambda c: (0, c)),
        out_shape=jax.ShapeDtypeStruct((rows, model), bf16),
        compiler_params=pltpu.CompilerParams(vmem_limit_bytes=48 * 1024 * 1024),
        cost_estimate=LARGE,
        name="feed_out",
    )(hidden, weights)


def input_back_kernel(q_width, kv_width, odd, dq, kept, first, second, last, cos_t, sin_t, w, dkv, dnormed):
    near = jnp.where(odd[0] == 0, first[0].astype(f32), second[0].astype(f32))
    total = kept[0].astype(f32) + near + last[...].astype(f32)
    cos_part, sin_part = cos_t[...], sin_t[...]
    parts = []
    for h in range(kv_width // HD):
        lead = total[h * HD:h * HD + HALF]
        trail = total[h * HD + HALF:(h + 1) * HD]
        parts += [
            (lead * cos_part + trail * sin_part).astype(bf16),
            (trail * cos_part - lead * sin_part).astype(bf16),
        ]
    parts.append(total[kv_width:].astype(bf16))
    rows = jnp.concatenate(parts, axis=0).T
    dkv[...] = rows
    low = nt(dq[...], w[:, :q_width]) + nt(rows, w[:, q_width:q_width + 2 * kv_width])
    dnormed[...] = low.astype(bf16)


def input_back(dq, odd, kept, arrived, last, cos_t, sin_t, weights):
    rows, q_width = dq.shape
    kv_width = kept.shape[1] // 2
    model = weights.shape[0]
    tile = 256
    table = pl.BlockSpec((HALF, tile), lambda r: (0, r))
    piece = lambda at: pl.BlockSpec((1, 2 * kv_width, tile), lambda r: (at, 0, r))
    return pl.pallas_call(
        functools.partial(input_back_kernel, q_width, kv_width),
        grid=(rows // tile,),
        in_specs=[
            pl.BlockSpec(memory_space=pltpu.SMEM),
            pl.BlockSpec((tile, q_width), lambda r: (r, 0)),
            piece(0),
            piece(0),
            piece(1),
            pl.BlockSpec((2 * kv_width, tile), lambda r: (0, r)),
            table,
            table,
            pl.BlockSpec(weights.shape, lambda r: (0, 0)),
        ],
        out_specs=[
            pl.BlockSpec((tile, 2 * kv_width), lambda r: (r, 0)),
            pl.BlockSpec((tile, model), lambda r: (r, 0)),
        ],
        out_shape=[
            jax.ShapeDtypeStruct((rows, 2 * kv_width), bf16),
            jax.ShapeDtypeStruct((rows, model), bf16),
        ],
        compiler_params=pltpu.CompilerParams(vmem_limit_bytes=48 * 1024 * 1024),
        cost_estimate=LARGE,
        name="input_back",
    )(odd, dq, kept, arrived, arrived, last, cos_t, sin_t, weights)


def output_kernel(stream, feed, other, before, out):
    out[0] = stream[...] + feed[...].astype(f32) + other[...].astype(f32)


def finish_output(other, stream, feed, part, parts, before):
    rows, model = stream.shape
    tile = 256
    block = pl.BlockSpec((tile, model), lambda r: (r, 0))
    return pl.pallas_call(
        output_kernel,
        grid=(rows // tile,),
        in_specs=[block, block, block, pl.BlockSpec(memory_space=pl.ANY)],
        out_specs=pl.BlockSpec((1, tile, model), lambda r: (part, r, 0)),
        out_shape=jax.ShapeDtypeStruct((parts, rows, model), f32),
        input_output_aliases={3: 0} if before.ndim == 3 else {},
        compiler_params=pltpu.CompilerParams(vmem_limit_bytes=32 * 1024 * 1024),
        cost_estimate=LARGE,
        name="finish_output",
    )(stream, feed, other, before)


def input_kernel(dstream, x, own, other, gain, before, out):
    values = x[...].astype(f32)
    inverse = lax.rsqrt(jnp.mean(values * values, axis=-1, keepdims=True) + norm_eps)
    unit = values * inverse
    scaled = gain[...] * (own[...].astype(f32) + other[...].astype(f32))
    back = inverse * (scaled - unit * jnp.mean(scaled * unit, axis=-1, keepdims=True))
    out[0] = dstream[...] + back


def finish_input(other, dstream, x, own, gain, part, parts, before):
    rows, model = dstream.shape
    tile = 256
    block = pl.BlockSpec((tile, model), lambda r: (r, 0))
    return pl.pallas_call(
        input_kernel,
        grid=(rows // tile,),
        in_specs=[block] * 4
        + [pl.BlockSpec((1, model), lambda r: (0, 0)), pl.BlockSpec(memory_space=pl.ANY)],
        out_specs=pl.BlockSpec((1, tile, model), lambda r: (part, r, 0)),
        out_shape=jax.ShapeDtypeStruct((parts, rows, model), f32),
        input_output_aliases={5: 0} if before.ndim == 3 else {},
        compiler_params=pltpu.CompilerParams(vmem_limit_bytes=32 * 1024 * 1024),
        cost_estimate=LARGE,
        name="finish_input",
    )(dstream, x, own, other, gain, before)


def interleave(gate, up):
    rows, ff = gate.shape
    pair = jnp.stack([gate.reshape(rows, -1, FF_TILE), up.reshape(rows, -1, FF_TILE)], axis=2)
    return pair.reshape(rows, 2 * ff)


def exchange(values, axis, step):
    size = lax.axis_size(axis)
    return lax.ppermute(values, axis, [(i, i ^ step) for i in range(size)])


def swap(values):
    return exchange(values, TP, 1)


def ring_blocks(block):
    size = lax.axis_size(CX)
    blocks = [block]
    for _ in range(size - 1):
        blocks.append(lax.ppermute(blocks[-1], CX, [(i, (i + 1) % size) for i in range(size)]))
    return blocks


def add_low(a, b):
    return (a.astype(f32) + b.astype(f32)).astype(bf16)


def after(value, *earlier):
    return lax.optimization_barrier((value,) + earlier)[0]


class Line:
    def __init__(self):
        self.last = ()

    def put(self, function, first, *rest):
        first = lax.optimization_barrier((first,) + self.last)[0]
        result = function(first, *rest)
        self.last = (jax.tree.leaves(result)[0],)
        return result


def core_add(kept, arrived):
    half = kept.shape[0] // 2
    return add_low(kept[half:], arrived[half:]), add_low(kept[:half], arrived[:half])


def copy_kernel(source, out):
    out[...] = source[...]


def copy_out(values):
    return pl.pallas_call(
        copy_kernel,
        out_shape=jax.ShapeDtypeStruct(values.shape, values.dtype),
        cost_estimate=LARGE,
        name="copy_out",
    )(values)


def near_pick(held, low):
    grid = held.reshape(2, 2, held.shape[0] // 4, held.shape[1])
    return lax.dynamic_index_in_dim(grid, low, axis=1, keepdims=False)


def far_pick(pair, high):
    return lax.dynamic_index_in_dim(pair, high, axis=0, keepdims=False)


def line_add(held, arrived):
    total = add_low(held, arrived)
    low = lax.axis_index(CX) % 2
    return near_pick(total, 1 - low), near_pick(total, low)


def near_add(held, arrived):
    total = add_low(held, arrived)
    high = lax.axis_index(CX) // 2
    return far_pick(total, 1 - high), far_pick(total, high)


def far_add(held, arrived):
    return held.astype(f32) + arrived.astype(f32)


def far_part(kept, arrived, odd):
    return add_low(kept[1], jnp.where(odd[0] == 0, arrived[1], arrived[0]))


def join(left, right):
    return tuple(jnp.concatenate(each, axis=1) for each in zip(left, right))


def body(
    tokens, out_grad, span_order,
    query_weight, key_weight, value_projection, output_weight, gate_weight, up_weight, down_weight,
    attention_gain, feedforward_gain, *moments,
):
    moments_one, moments_two = moments[:9], moments[9:]
    shards_axes = (DP, CX)
    sequence_count, sequence_rows, model = tokens.shape
    q_width, kv_width = query_weight.shape[1], key_weight.shape[1]
    ff = gate_weight.shape[1]
    context_size = lax.axis_size(CX)
    span_rows = sequence_rows // 2
    gains_low = jnp.stack([attention_gain, feedforward_gain], axis=1).astype(bf16)

    first_shard = jnp.concatenate(
        [
            query_weight.astype(bf16),
            key_weight.astype(bf16),
            value_projection.astype(bf16),
            jnp.pad(gains_low, ((0, 0), (0, 126))),
        ],
        axis=1,
    )
    head_w = lax.all_gather(first_shard, shards_axes, axis=0, tiled=True)
    out_shard = output_weight.astype(bf16).T
    out_w = lax.all_gather(
        after(jnp.concatenate([out_shard, swap(out_shard)], axis=1), head_w), shards_axes, axis=0, tiled=True
    )
    second_shard = jnp.concatenate(
        [interleave(gate_weight.astype(bf16), up_weight.astype(bf16)), down_weight.astype(bf16).T],
        axis=1,
    )
    gains = head_w[:, q_width + 2 * kv_width:q_width + 2 * kv_width + 2].astype(f32).T
    mixer_scale, forward_scale = gains[0:1], gains[1:2]

    context_index = lax.axis_index(CX)
    ring_slots = jnp.stack(
        [2 * ((context_index - s) % context_size) + t for s in range(context_size) for t in range(2)]
    )
    ring_spans = span_order[ring_slots]
    spans = jnp.concatenate([ring_spans[:2], ring_spans]).astype(jnp.int32)
    positions = (
        spans[:2, None] * span_rows + jnp.arange(span_rows, dtype=jnp.int32)[None, :]
    ).reshape(sequence_rows)
    frequency = rope_base ** (-(jnp.arange(HALF, dtype=f32) * 2.0) / HEAD_DIMENSION)
    angles = frequency[:, None] * positions.astype(f32)[None, :]
    cos_t, sin_t = jnp.cos(angles), jnp.sin(angles)
    odd = (context_index % 2).astype(jnp.int32).reshape(1)
    device = lax.axis_index(DP)
    core, line = device % 2, device // 2
    order = jnp.stack(
        [line * 2 + core, (1 - line) * 2 + core, line * 2 + 1 - core, (1 - line) * 2 + 1 - core]
    ).astype(jnp.int32)

    sequences = range(sequence_count)
    normed_one, queries, blocks = [], [], []
    for s in sequences:
        n1, qt, kv = project(tokens[s], mixer_scale, head_w, cos_t, sin_t, q_width, kv_width)
        normed_one.append(n1)
        queries.append(qt)
        blocks.append(ring_blocks(kv))
    rest_w = lax.all_gather(
        after(second_shard, *[each[0] for each in blocks]), shards_axes, axis=0, tiled=True
    )
    attended = [attention_forward(spans, queries[s], blocks[s]) for s in sequences]
    streams, normed_two = [], []
    for s in sequences:
        own = attended[s][0]
        stream, n2 = mix_heads(tokens[s], own, swap(own), forward_scale, out_w, 0)
        streams.append(stream)
        normed_two.append(n2)
    line = Line()
    hiddens, dboths, dnormed, others = [], [], [], []
    for s in sequences:
        hidden, dboth, dn2 = line.put(feed_forward, normed_two[s], out_grad[s], rest_w, ff)
        hiddens.append(hidden)
        dboths.append(dboth)
        dnormed.append(dn2)
        others.append(swap(line.put(copy_out, dn2)))

    def back(s):
        return line.put(
            stream_back, others[s], streams[s], out_grad[s], dnormed[s], forward_scale, out_w, 0, q_width
        )

    def attend_back(s, dheads):
        return line.put(
            attention_backward, dheads, spans, queries[s], attended[s][1], attended[s][2], cos_t, sin_t, blocks[s]
        )

    grads = lambda left, right, tile: line.put(gradient, left, right, order, tile)
    masters = (
        query_weight, key_weight, value_projection, output_weight, gate_weight, up_weight, down_weight,
        attention_gain, feedforward_gain,
    )
    full_rows = span_order.shape[0] * span_rows
    matrix_rate = 1.0 / math.sqrt(MODEL_DIMENSION)
    output_rate = 1.0 / math.sqrt(8 * QUERY_HEADS * HEAD_DIMENSION // full_rows)
    rates = (matrix_rate,) * 3 + (output_rate,) + (matrix_rate,) * 3 + (gain_rate,) * 2
    decays = (decay_rate,) * 7 + (0.0,) * 2

    def update(at, shard):
        return (shard,) + adamw_update(
            masters[at], shard, moments_one[at], moments_two[at], rates[at], decays[at]
        )

    def finish_down(mine, far):
        return (update(6, far_add(mine, far).T),)

    def finish_both(mine, far):
        total = far_add(mine, far)
        pair = total.reshape(total.shape[0], -1, 2, FF_TILE)
        sums = jnp.sum(total * second_shard[:, :2 * ff].astype(f32), axis=1)
        return update(4, pair[:, :, 0].reshape(-1, ff)), update(5, pair[:, :, 1].reshape(-1, ff)), sums

    def finish_mid(mine, far):
        total = far_add(mine, far)
        query = total[:, q_width:]
        sums = jnp.sum(query * first_shard[:, :q_width].astype(f32), axis=1)
        return update(0, query), update(3, total[:, :q_width].T), sums

    def finish_kv(mine, far):
        total = far_add(mine, far)
        sums = jnp.sum(total * first_shard[:, q_width:q_width + 2 * kv_width].astype(f32), axis=1)
        return update(1, total[:, :kv_width]), update(2, total[:, kv_width:]), sums

    down_kept, down_sent = grads([out_grad[s] for s in sequences], hiddens, GRAD_TILE)
    down_core = exchange(down_sent, DP, 1)
    dstream_a, dlow_a, dheads_a = back(0)
    down_passed, down_held = line.put(core_add, down_kept, down_core)
    down_line = exchange(down_passed, DP, 2)
    dq_a, kept_a, sent_a = attend_back(0, dheads_a)
    arrived_a = exchange(line.put(copy_out, sent_a), CX, 1)
    both_kept, both_sent = grads(normed_two, dboths, GRAD_TILE)
    both_core = exchange(both_sent, DP, 1)
    dstream_b, dlow_b, dheads_b = back(1)
    both_passed, both_held = line.put(core_add, both_kept, both_core)
    both_line = exchange(both_passed, DP, 2)
    last_a = exchange(line.put(far_part, kept_a, arrived_a, odd), CX, 2)
    down_away, down_mine = line.put(line_add, down_held, down_line)
    down_near = exchange(down_away, CX, 1)
    dq_b, kept_b, sent_b = attend_back(1, dheads_b)
    arrived_b = exchange(line.put(copy_out, sent_b), CX, 1)
    feed_a = line.put(feed_out, hiddens[0], rest_w, 2 * ff)
    feed_other_a = swap(feed_a)
    down_away, down_mine = line.put(near_add, down_mine, down_near)
    down_far = exchange(down_away, CX, 2)
    dkv_a, dn1_a = line.put(input_back, dq_a, odd, kept_a, arrived_a, last_a, cos_t, sin_t, head_w)
    dn1_other_a = swap(line.put(copy_out, dn1_a))
    output_parts = grads([dlow_a, dlow_b], [each[0] for each in attended], q_width)
    query_parts = grads(normed_one, [dq_a, dq_b], q_width)
    mid_kept, mid_sent = line.put(join, output_parts, query_parts)
    mid_core = exchange(mid_sent, DP, 1)
    last_b = exchange(line.put(far_part, kept_b, arrived_b, odd), CX, 2)
    output_field = line.put(finish_output, feed_other_a, streams[0], feed_a, 0, sequence_count, order)
    mid_passed, mid_held = line.put(core_add, mid_kept, mid_core)
    mid_line = exchange(mid_passed, DP, 2)
    (down_done,) = line.put(finish_down, down_mine, down_far)
    both_away, both_mine = line.put(line_add, both_held, both_line)
    both_near = exchange(both_away, CX, 1)
    dkv_b, dn1_b = line.put(input_back, dq_b, odd, kept_b, arrived_b, last_b, cos_t, sin_t, head_w)
    kv_kept, kv_sent = grads(normed_one, [dkv_a, dkv_b], 2 * kv_width)
    kv_core = exchange(kv_sent, DP, 1)
    dn1_other_b = swap(line.put(copy_out, dn1_b))
    input_field = line.put(
        finish_input, dn1_other_a, dstream_a, tokens[0], dn1_a, mixer_scale, 0, sequence_count, order
    )
    kv_passed, kv_held = line.put(core_add, kv_kept, kv_core)
    kv_line = exchange(kv_passed, DP, 2)
    mid_away, mid_mine = line.put(line_add, mid_held, mid_line)
    mid_near = exchange(mid_away, CX, 1)
    feed_b = line.put(feed_out, hiddens[1], rest_w, 2 * ff)
    feed_other_b = swap(feed_b)
    both_away, both_mine = line.put(near_add, both_mine, both_near)
    both_far = exchange(both_away, CX, 2)
    kv_away, kv_mine = line.put(line_add, kv_held, kv_line)
    kv_near = exchange(kv_away, CX, 1)
    mid_away, mid_mine = line.put(near_add, mid_mine, mid_near)
    mid_far = exchange(mid_away, CX, 2)
    input_field = line.put(
        finish_input, dn1_other_b, dstream_b, tokens[1], dn1_b, mixer_scale, 1, sequence_count, input_field
    )
    kv_away, kv_mine = line.put(near_add, kv_mine, kv_near)
    kv_far = exchange(kv_away, CX, 2)
    gate_done, up_done, both_sums = line.put(finish_both, both_mine, both_far)
    output_field = line.put(
        finish_output, feed_other_b, streams[1], feed_b, 1, sequence_count, output_field
    )
    query_done, output_done, query_sums = line.put(finish_mid, mid_mine, mid_far)
    key_done, value_done, kv_sums = line.put(finish_kv, kv_mine, kv_far)
    row_sums = jnp.stack([query_sums + kv_sums, both_sums])
    gain_shard = (row_sums + swap(row_sums)) / gains_low.astype(f32).T
    done = (
        query_done, key_done, value_done, output_done, gate_done, up_done, down_done,
        update(7, gain_shard[0]), update(8, gain_shard[1]),
    )
    return (output_field, input_field) + tuple(each[part] for part in range(4) for each in done)


def solution(mesh):
    rows, cols, gains = P((DP, CX), TP), P(TP, (DP, CX)), P((DP, CX))
    stream = P(DP, CX, None)
    params = (rows,) * 3 + (cols,) + (rows,) * 2 + (cols,) + (gains,) * 2
    fast = (
        mesh.shape[TP] == 2
        and mesh.shape[DP] == 4
        and mesh.shape[CX] == 4
        and (KEY_VALUE_HEADS // 2 * HEAD_DIMENSION) % 128 == 0
    )
    return jax.shard_map(
        body if fast else plain_body,
        mesh=mesh,
        in_specs=(stream, stream, P()) + params * 3,
        out_specs=(stream, stream) + params * 4,
        check_vma=False,
    )
```

```python
import functools
import math

import jax
import jax.numpy as jnp
from jax import lax
from jax.experimental import pallas as pl
from jax.experimental.pallas import tpu as pltpu
from jax.sharding import PartitionSpec as P

MODEL_DIMENSION = 1536
QUERY_HEADS = 16
KEY_VALUE_HEADS = 8
HEAD_DIMENSION = 96
FF_TILE = 512
GRAD_TILE = 1024
SMALL = pl.CostEstimate(flops=1000, bytes_accessed=1000, transcendentals=0)
LARGE = pl.CostEstimate(flops=10**12, bytes_accessed=1000, transcendentals=0)
DP, CX, TP = "dp", "context", "tensor"


norm_eps = 1e-05
rope_base = 100000.0
beta_one = 0.9
beta_two = 0.95
adam_eps = 1e-08
gain_rate = 0.6
decay_rate = 0.1
step_count = 4.0


HD = HEAD_DIMENSION
HALF = 48
LOG2E = 1.4426950408889634
f32 = jnp.float32
bf16 = jnp.bfloat16

def nn(a, b):
    return lax.dot_general(a, b, (((1,), (0,)), ((), ())), preferred_element_type=f32)

def nt(a, b):
    return lax.dot_general(a, b, (((1,), (1,)), ((), ())), preferred_element_type=f32)

def spread_heads(kv_refs, k_heads, kv_heads, rows, base):
    for s, ref in enumerate(kv_refs):
        for h in range(kv_heads):
            k_heads[h, s * rows:(s + 1) * rows, :] = ref[:, base + h * HD: base + (h + 1) * HD]

def forward_kernel(kv_heads, group, span_rows, spans, qt, *refs):
    blocks = len(refs) - 3 - 6
    kv_refs = refs[:blocks]
    out_low, out_t, log_total = refs[blocks:blocks + 3]
    k_heads, v_t, q_wide, top, total, acc = refs[blocks + 3:]
    rows = kv_refs[0].shape[0]
    kv_width = kv_heads * HD
    wide = group * span_rows
    scale = LOG2E / math.sqrt(HD)
    spread_heads(kv_refs, k_heads, kv_heads, rows, 0)
    for s, ref in enumerate(kv_refs):
        v_t[:, s * rows:(s + 1) * rows] = ref[:, kv_width:].T
    for h in range(kv_heads):
        for i in range(2):
            q_wide[h, i] = jnp.concatenate(
                [qt[(h * group + n) * HD:(h * group + n + 1) * HD, i * span_rows:(i + 1) * span_rows]
                 for n in range(group)], axis=1)
    key_at = lax.broadcasted_iota(jnp.int32, (span_rows, wide), 0)
    query_at = lax.broadcasted_iota(jnp.int32, (span_rows, wide), 1) % span_rows
    keep = key_at <= query_at
    for i in range(2):
        for h in range(kv_heads):
            scores = nn(k_heads[h, i * span_rows:(i + 1) * span_rows, :], q_wide[h, i]) * scale
            scores = jnp.where(keep, scores, -1e30)
            peak = jnp.max(scores, axis=0, keepdims=True)
            probs = jnp.exp2(scores - peak)
            top[h, i] = peak
            total[h, i] = jnp.sum(probs, axis=0, keepdims=True)
            acc[h, i] = nn(v_t[h * HD:(h + 1) * HD, i * span_rows:(i + 1) * span_rows], probs.astype(bf16))

    def visit(j, _):
        start = pl.multiple_of(j * span_rows, span_rows)
        for i in range(2):
            @pl.when(spans[2 + j] < spans[i])
            def _():
                for h in range(kv_heads):
                    scores = nn(k_heads[h, pl.ds(start, span_rows), :], q_wide[h, i]) * scale
                    before = top[h, i]
                    peak = jnp.maximum(before, jnp.max(scores, axis=0, keepdims=True))
                    fade = jnp.exp2(before - peak)
                    probs = jnp.exp2(scores - peak)
                    top[h, i] = peak
                    total[h, i] = total[h, i] * fade + jnp.sum(probs, axis=0, keepdims=True)
                    acc[h, i] = acc[h, i] * fade + nn(
                        v_t[h * HD:(h + 1) * HD, pl.ds(start, span_rows)], probs.astype(bf16))
        return 0
    lax.fori_loop(0, 2 * blocks, visit, 0)
    for i in range(2):
        cols = slice(i * span_rows, (i + 1) * span_rows)
        for h in range(kv_heads):
            sums = total[h, i]
            whole = (acc[h, i] / sums).astype(bf16)
            level = top[h, i] + jnp.log2(sums)
            for n in range(group):
                at = h * group + n
                lanes = slice(n * span_rows, (n + 1) * span_rows)
                out_t[at * HD:(at + 1) * HD, cols] = whole[:, lanes]
                log_total[at:at + 1, cols] = level[:, lanes]
    out_low[...] = out_t[...].T

def attention_forward(spans, qt, kv_blocks):
    width, rows = qt.shape
    kv_heads = kv_blocks[0].shape[1] // (2 * HD)
    heads = width // HD
    group = heads // kv_heads
    span_rows = rows // 2
    keys = rows * len(kv_blocks)
    wide = group * span_rows
    whole = lambda: pl.BlockSpec(memory_space=pltpu.VMEM)
    return pl.pallas_call(
        functools.partial(forward_kernel, kv_heads, group, span_rows),
        in_specs=[pl.BlockSpec(memory_space=pltpu.SMEM)] + [whole() for _ in range(1 + len(kv_blocks))],
        out_specs=[whole(), whole(), whole()],
        out_shape=[jax.ShapeDtypeStruct((rows, width), bf16), jax.ShapeDtypeStruct((width, rows), bf16),
                   jax.ShapeDtypeStruct((heads, rows), f32)],
        scratch_shapes=[pltpu.VMEM((kv_heads, keys, HD), bf16), pltpu.VMEM((kv_heads * HD, keys), bf16),
                        pltpu.VMEM((kv_heads, 2, HD, wide), bf16), pltpu.VMEM((kv_heads, 2, 1, wide), f32),
                        pltpu.VMEM((kv_heads, 2, 1, wide), f32), pltpu.VMEM((kv_heads, 2, HD, wide), f32)],
        compiler_params=pltpu.CompilerParams(vmem_limit_bytes=48 * 1024 * 1024),
        cost_estimate=SMALL,
        name="attention_forward",
    )(spans, qt, *kv_blocks)

def backward_kernel(kv_heads, group, span_rows, blocks, spans, qt, dot_, out_t, log_total, cos_t, sin_t, *refs):
    kv_refs = refs[:blocks]
    dq_low, kept, sent = refs[blocks:blocks + 3]
    k_heads, v_heads, k_t, q_wide, d_wide, level, inner, dq_acc, dk_acc, dv_acc = refs[blocks + 3:]
    rows = kv_refs[0].shape[0]
    kv_width = kv_heads * HD
    wide = group * span_rows
    scale = 1.0 / math.sqrt(HD)
    spread_heads(kv_refs, k_heads, kv_heads, rows, 0)
    spread_heads(kv_refs, v_heads, kv_heads, rows, kv_width)
    for s, ref in enumerate(kv_refs):
        k_t[:, s * rows:(s + 1) * rows] = ref[:, :kv_width].T
    for h in range(kv_heads):
        for i in range(2):
            cols = slice(i * span_rows, (i + 1) * span_rows)
            heads = [slice((h * group + n) * HD, (h * group + n + 1) * HD) for n in range(group)]
            q_wide[h, i] = jnp.concatenate([qt[at, cols] for at in heads], axis=1)
            d_wide[h, i] = jnp.concatenate([dot_[at, cols] for at in heads], axis=1)
            level[h, i] = jnp.concatenate([log_total[h * group + n:h * group + n + 1, cols] for n in range(group)], axis=1)
            inner[h, i] = jnp.concatenate(
                [jnp.sum(dot_[at, cols].astype(f32) * out_t[at, cols].astype(f32), axis=0, keepdims=True) for at in heads], axis=1)
    dk_acc[...] = jnp.zeros_like(dk_acc)
    dv_acc[...] = jnp.zeros_like(dv_acc)
    key_at = lax.broadcasted_iota(jnp.int32, (span_rows, wide), 0)
    query_at = lax.broadcasted_iota(jnp.int32, (span_rows, wide), 1) % span_rows
    keep = key_at <= query_at

    def pair(h, i, at, masked):
        scores = nn(k_heads[h, at, :], q_wide[h, i]) * (scale * LOG2E)
        probs = jnp.exp2(scores - level[h, i])
        if masked:
            probs = jnp.where(keep, probs, 0.0)
        dprobs = nn(v_heads[h, at, :], d_wide[h, i])
        dscores = (probs * (dprobs - inner[h, i])).astype(bf16)
        head = slice(h * HD, (h + 1) * HD)
        dv_acc[head, at] += nt(d_wide[h, i], probs.astype(bf16))
        dk_acc[head, at] += nt(q_wide[h, i], dscores)
        step = nn(k_t[head, at], dscores)
        if masked:
            dq_acc[h, i] = step
        else:
            dq_acc[h, i] += step

    for i in range(2):
        for h in range(kv_heads):
            pair(h, i, slice(i * span_rows, (i + 1) * span_rows), True)

    def visit(j, _):
        start = pl.multiple_of(j * span_rows, span_rows)
        for i in range(2):
            @pl.when(spans[2 + j] < spans[i])
            def _():
                for h in range(kv_heads):
                    pair(h, i, pl.ds(start, span_rows), False)
        return 0
    lax.fori_loop(0, 2 * blocks, visit, 0)
    for i in range(2):
        cols = slice(i * span_rows, (i + 1) * span_rows)
        cos_part, sin_part = cos_t[:, cols], sin_t[:, cols]
        parts = []
        for h in range(kv_heads):
            for n in range(group):
                grad = dq_acc[h, i, :, n * span_rows:(n + 1) * span_rows] * scale
                lead, trail = grad[:HALF], grad[HALF:]
                parts += [(lead * cos_part + trail * sin_part).astype(bf16), (trail * cos_part - lead * sin_part).astype(bf16)]
        dq_low[cols, :] = jnp.concatenate(parts, axis=0).T
    for s in range(blocks):
        cols = slice(s * rows, (s + 1) * rows)
        ref = (kept, sent)[s % 2]
        ref[s // 2, :kv_width, :] = (dk_acc[:, cols] * scale).astype(bf16)
        ref[s // 2, kv_width:, :] = dv_acc[:, cols].astype(bf16)

def attention_backward(dot_, spans, qt, out_t, log_total, cos_t, sin_t, kv_blocks):
    width, rows = qt.shape
    kv_heads = kv_blocks[0].shape[1] // (2 * HD)
    heads = width // HD
    group = heads // kv_heads
    span_rows = rows // 2
    blocks = len(kv_blocks)
    keys = rows * blocks
    wide = group * span_rows
    kv_width = kv_heads * HD
    whole = lambda: pl.BlockSpec(memory_space=pltpu.VMEM)
    return pl.pallas_call(
        functools.partial(backward_kernel, kv_heads, group, span_rows, blocks),
        in_specs=[pl.BlockSpec(memory_space=pltpu.SMEM)] + [whole() for _ in range(6 + blocks)],
        out_specs=[whole() for _ in range(3)],
        out_shape=[jax.ShapeDtypeStruct((rows, width), bf16)] + [jax.ShapeDtypeStruct((blocks // 2, 2 * kv_width, rows), bf16)] * 2,
        scratch_shapes=[pltpu.VMEM((kv_heads, keys, HD), bf16), pltpu.VMEM((kv_heads, keys, HD), bf16),
                        pltpu.VMEM((kv_width, keys), bf16),
                        pltpu.VMEM((kv_heads, 2, HD, wide), bf16), pltpu.VMEM((kv_heads, 2, HD, wide), bf16),
                        pltpu.VMEM((kv_heads, 2, 1, wide), f32), pltpu.VMEM((kv_heads, 2, 1, wide), f32),
                        pltpu.VMEM((kv_heads, 2, HD, wide), f32),
                        pltpu.VMEM((kv_width, keys), f32), pltpu.VMEM((kv_width, keys), f32)],
        compiler_params=pltpu.CompilerParams(vmem_limit_bytes=56 * 1024 * 1024),
        cost_estimate=LARGE,
        name="attention_backward",
    )(spans, qt, dot_, out_t, log_total, cos_t, sin_t, *kv_blocks)

def project_kernel(q_width, kv_width, x, gain, w, cos_t, sin_t, n1, qt, kv):
    values = x[...].astype(f32)
    inverse = lax.rsqrt(jnp.mean(values * values, axis=-1, keepdims=True) + 1e-05)
    normed = (values * inverse * gain[...]).astype(bf16)
    n1[...] = normed
    both = nn(normed, w[:, :q_width + kv_width])
    rows = both.shape[0]
    turned = both.T
    cos_part, sin_part = cos_t[...], sin_t[...]
    parts = []
    for h in range((q_width + kv_width) // HD):
        lead = turned[h * HD:h * HD + HALF]
        trail = turned[h * HD + HALF:(h + 1) * HD]
        parts += [(lead * cos_part - trail * sin_part).astype(bf16), (trail * cos_part + lead * sin_part).astype(bf16)]
    cut = q_width // HALF
    qt[...] = jnp.concatenate(parts[:cut], axis=0)
    kv[:, :kv_width] = jnp.concatenate(parts[cut:], axis=0).T
    kv[:, kv_width:] = nn(normed, w[:, q_width + kv_width:q_width + 2 * kv_width]).astype(bf16)

def project(x, gain, w, cos_t, sin_t, q_width, kv_width):
    rows, model = x.shape
    tile = 256
    return pl.pallas_call(
        functools.partial(project_kernel, q_width, kv_width),
        grid=(rows // tile,),
        in_specs=[pl.BlockSpec((tile, model), lambda r: (r, 0)),
                  pl.BlockSpec((1, model), lambda r: (0, 0)),
                  pl.BlockSpec((model, w.shape[1]), lambda r: (0, 0)),
                  pl.BlockSpec((HALF, tile), lambda r: (0, r)),
                  pl.BlockSpec((HALF, tile), lambda r: (0, r))],
        out_specs=[pl.BlockSpec((tile, model), lambda r: (r, 0)),
                   pl.BlockSpec((q_width, tile), lambda r: (0, r)),
                   pl.BlockSpec((tile, 2 * kv_width), lambda r: (r, 0))],
        out_shape=[jax.ShapeDtypeStruct((rows, model), bf16), jax.ShapeDtypeStruct((q_width, rows), bf16),
                   jax.ShapeDtypeStruct((rows, 2 * kv_width), bf16)],
        compiler_params=pltpu.CompilerParams(vmem_limit_bytes=48 * 1024 * 1024),
        cost_estimate=SMALL,
        name="project_heads",
    )(x, gain, w, cos_t, sin_t)


def rotate(values, cosine, sine_part):
    halfway = values.shape[-1] // 2
    leading = values[..., :halfway]
    trailing = values[..., halfway:]
    return jnp.concatenate(
        [leading * cosine - trailing * sine_part, trailing * cosine + leading * sine_part], axis=-1
    )


def rotate_back(values, cosine, sine_part):
    halfway = values.shape[-1] // 2
    leading = values[..., :halfway]
    trailing = values[..., halfway:]
    return jnp.concatenate(
        [leading * cosine + trailing * sine_part, trailing * cosine - leading * sine_part], axis=-1
    )


def norm_back(values, inverse, gain, upstream):
    scaled = gain * upstream
    unit_rows = values * inverse
    result = inverse * (scaled - unit_rows * jnp.mean(scaled * unit_rows, axis=-1, keepdims=True))
    return (result, jnp.sum(upstream * unit_rows, axis=0))


def contract_rows(left_side, right_side):
    return lax.dot_general(
        left_side, right_side, (((0,), (0,)), ((), ())), preferred_element_type=jnp.float32
    )


def contract_cols(left_side, right_side):
    return lax.dot_general(
        left_side, right_side, (((1,), (1,)), ((), ())), preferred_element_type=jnp.float32
    )


def adamw_update(weight, gradient, moment_one, moment_two, rate_value, decay_value):
    first_new = beta_one * moment_one + (1.0 - beta_one) * gradient
    second_new = beta_two * moment_two + (1.0 - beta_two) * gradient * gradient
    corrected = (
        first_new
        / (1.0 - beta_one**step_count)
        / (jnp.sqrt(second_new / (1.0 - beta_two**step_count)) + adam_eps)
    )
    return (weight - rate_value * (corrected + decay_value * weight), first_new, second_new)


def plain_body(
    tokens,
    out_grad,
    span_order,
    query_weight,
    key_weight,
    value_projection,
    output_weight,
    gate_weight,
    up_weight,
    down_weight,
    attention_gain,
    feedforward_gain,
    query_weight_first,
    key_projection_first_moment,
    value_projection_first_moment,
    output_weight_first,
    gate_weight_first,
    up_weight_first,
    down_weight_first,
    attention_gain_first,
    feedforward_gain_first,
    query_weight_second,
    key_projection_second_moment,
    value_projection_second_moment,
    output_weight_second,
    gate_weight_second,
    up_weight_second,
    down_weight_second,
    attention_gain_second,
    feedforward_gain_second,
):
    bf16 = jnp.bfloat16
    f32 = jnp.float32
    gathered = (
        lax.all_gather(query_weight.astype(bf16), (DP, CX), axis=0, tiled=True),
        lax.all_gather(key_weight.astype(bf16), (DP, CX), axis=0, tiled=True),
        lax.all_gather(value_projection.astype(bf16), (DP, CX), axis=0, tiled=True),
        lax.all_gather(output_weight.astype(bf16), (DP, CX), axis=1, tiled=True),
        lax.all_gather(gate_weight.astype(bf16), (DP, CX), axis=0, tiled=True),
        lax.all_gather(up_weight.astype(bf16), (DP, CX), axis=0, tiled=True),
        lax.all_gather(down_weight.astype(bf16), (DP, CX), axis=1, tiled=True),
        lax.all_gather(attention_gain.astype(bf16), (DP, CX), axis=0, tiled=True),
        lax.all_gather(feedforward_gain.astype(bf16), (DP, CX), axis=0, tiled=True),
    )
    (
        query_matrix,
        projected_keys,
        projected_values,
        output_matrix,
        gate_matrix,
        up_matrix,
        down_matrix,
        mixer_gain,
        forward_gain,
    ) = gathered
    sequence_count, sequence_rows, model_width = tokens.shape
    token_count = sequence_count * sequence_rows
    tensor_size = lax.axis_size(TP)
    own_rows = token_count // tensor_size
    span_rows = sequence_rows // 2
    span_total = span_order.shape[0]
    full_rows = span_total * span_rows
    local_heads = query_matrix.shape[1] // HEAD_DIMENSION
    kv_heads = projected_keys.shape[1] // HEAD_DIMENSION
    query_group_width = local_heads // kv_heads
    score_scale = 1.0 / math.sqrt(HEAD_DIMENSION)
    all_positions = (
        span_order[:, None] * span_rows + jnp.arange(span_rows, dtype=jnp.int32)[None, :]
    ).reshape(full_rows)
    context_index = lax.axis_index(CX)
    query_positions = lax.dynamic_slice_in_dim(
        all_positions, context_index * sequence_rows, sequence_rows
    )
    frequency = rope_base ** (-(jnp.arange(HEAD_DIMENSION // 2, dtype=f32) * 2.0) / HEAD_DIMENSION)
    angles = query_positions.astype(f32)[:, None] * frequency[None, :]
    cosine = jnp.cos(angles)[:, None, :]
    sine_part = jnp.sin(angles)[:, None, :]
    stream_in = tokens.astype(f32).reshape(token_count, model_width)
    inverse_one = lax.rsqrt(jnp.mean(stream_in * stream_in, axis=-1, keepdims=True) + norm_eps)
    mixer_scale = mixer_gain.astype(f32)
    first_normalized = (stream_in * inverse_one * mixer_scale).astype(bf16)
    query_raw = jnp.dot(first_normalized, query_matrix, preferred_element_type=f32).reshape(
        sequence_count, sequence_rows, local_heads, HEAD_DIMENSION
    )
    query_vectors = (
        rotate(query_raw, cosine, sine_part)
        .astype(bf16)
        .reshape(sequence_count, sequence_rows, kv_heads, query_group_width, HEAD_DIMENSION)
        .transpose(0, 2, 3, 1, 4)
    )
    unrotated_keys = jnp.dot(first_normalized, projected_keys, preferred_element_type=f32).reshape(
        sequence_count, sequence_rows, kv_heads, HEAD_DIMENSION
    )
    key_rows = (
        rotate(unrotated_keys, cosine, sine_part)
        .astype(bf16)
        .reshape(sequence_count, sequence_rows, kv_heads * HEAD_DIMENSION)
    )
    value_row_slice = (
        jnp.dot(first_normalized, projected_values, preferred_element_type=f32)
        .astype(bf16)
        .reshape(sequence_count, sequence_rows, kv_heads * HEAD_DIMENSION)
    )
    pieces = (
        lax.all_gather(key_rows, CX, axis=1, tiled=True),
        lax.all_gather(value_row_slice, CX, axis=1, tiled=True),
    )
    row_max = jnp.full((sequence_count, kv_heads, query_group_width, sequence_rows), -1e30, f32)
    piece_rows = pieces[0].shape[1]
    key_grid = pieces[0].reshape(sequence_count, piece_rows, kv_heads, HEAD_DIMENSION)
    value_grid = pieces[1].reshape(sequence_count, piece_rows, kv_heads, HEAD_DIMENSION)
    scores = (
        jnp.einsum("shgqd,skhd->shgqk", query_vectors, key_grid, preferred_element_type=f32)
        * score_scale
    )
    allowed = all_positions[None, :] <= query_positions[:, None]
    new_max = jnp.maximum(row_max, jnp.max(jnp.where(allowed, scores, -1e30), axis=-1))
    weights = jnp.where(allowed, jnp.exp(scores - new_max[..., None]), 0.0)
    row_total = jnp.sum(weights, axis=-1)
    summed = jnp.einsum(
        "shgqk,skhd->shgqd", weights.astype(bf16), value_grid, preferred_element_type=f32
    )
    row_max, row_total, summed = (new_max, row_total, summed)
    attention_out = summed / row_total[..., None]
    attention_low = (
        attention_out.transpose(0, 3, 1, 2, 4)
        .reshape(token_count, local_heads * HEAD_DIMENSION)
        .astype(bf16)
    )
    mixed_own = lax.psum_scatter(
        jnp.dot(attention_low, output_matrix, preferred_element_type=f32).astype(jnp.bfloat16),
        TP,
        scatter_dimension=0,
        tiled=True,
    ).astype(jnp.float32)
    tensor_index = lax.axis_index(TP)
    stream_own = (
        lax.dynamic_slice_in_dim(stream_in, tensor_index * own_rows, own_rows, 0) + mixed_own
    )
    stream_mid = lax.all_gather(
        stream_own.astype(jnp.bfloat16), TP, axis=0, tiled=True
    ).astype(stream_own.dtype)
    inverse_two = lax.rsqrt(jnp.mean(stream_mid * stream_mid, axis=-1, keepdims=True) + norm_eps)
    forward_scale = forward_gain.astype(f32)
    normed_two = (stream_mid * inverse_two * forward_scale).astype(bf16)
    gate_float = (
        jnp.dot(normed_two, gate_matrix, preferred_element_type=f32).astype(bf16).astype(f32)
    )
    up_float = jnp.dot(normed_two, up_matrix, preferred_element_type=f32).astype(bf16).astype(f32)
    sigmoid = jax.nn.sigmoid(gate_float)
    hidden = (gate_float * sigmoid * up_float).astype(bf16)
    feed_terms = jnp.dot(hidden, down_matrix, preferred_element_type=f32)
    feed_sum = lax.psum(feed_terms.astype(jnp.bfloat16), TP).astype(jnp.float32)
    output_field = (stream_mid + feed_sum).reshape(sequence_count, sequence_rows, model_width)
    upstream = out_grad.reshape(token_count, model_width)
    hidden_grad = contract_cols(upstream, down_matrix)
    down_grad = contract_rows(hidden, upstream)
    gate_grad_low = (
        hidden_grad * up_float * sigmoid * (1.0 + gate_float * (1.0 - sigmoid))
    ).astype(bf16)
    up_grad_low = (hidden_grad * gate_float * sigmoid).astype(bf16)
    gate_grad = contract_rows(normed_two, gate_grad_low)
    up_grad = contract_rows(normed_two, up_grad_low)
    normed_two_grad = lax.psum_scatter(
        (contract_cols(gate_grad_low, gate_matrix) + contract_cols(up_grad_low, up_matrix)).astype(
            jnp.bfloat16
        ),
        TP,
        scatter_dimension=0,
        tiled=True,
    ).astype(jnp.float32)
    inverse_own = lax.dynamic_slice_in_dim(inverse_two, tensor_index * own_rows, own_rows, 0)
    stream_back, forward_gain_part = norm_back(
        stream_own, inverse_own, forward_scale, normed_two_grad
    )
    stream_grad_own = (
        lax.dynamic_slice_in_dim(upstream, tensor_index * own_rows, own_rows, 0).astype(f32)
        + stream_back
    )
    stream_grad = lax.all_gather(
        stream_grad_own.astype(jnp.bfloat16), TP, axis=0, tiled=True
    ).astype(stream_grad_own.dtype)
    stream_grad_low = stream_grad.astype(bf16)
    output_grad = contract_rows(attention_low, stream_grad_low)
    attention_grad = contract_cols(stream_grad_low, output_matrix)
    head_grad = attention_grad.reshape(
        sequence_count, sequence_rows, kv_heads, query_group_width, HEAD_DIMENSION
    ).transpose(0, 2, 3, 1, 4)
    key_again, value_again = (
        lax.all_gather(key_rows, CX, axis=1, tiled=True),
        lax.all_gather(value_row_slice, CX, axis=1, tiled=True),
    )

    def sequence_back(element):
        query_seq, key_seq, value_seq, max_seq, total_seq, out_seq, grad_seq = element
        key_grid = key_seq.reshape(full_rows, kv_heads, HEAD_DIMENSION)
        value_grid = value_seq.reshape(full_rows, kv_heads, HEAD_DIMENSION)
        accum_grad = (grad_seq / total_seq[..., None]).astype(bf16)
        row_term = jnp.sum(grad_seq * out_seq, axis=-1) / total_seq
        scores = (
            jnp.einsum("hgqd,khd->hgqk", query_seq, key_grid, preferred_element_type=f32)
            * score_scale
        )
        allowed = all_positions[None, :] <= query_positions[:, None]
        weights = jnp.where(allowed, jnp.exp(scores - max_seq[..., None]), 0.0)
        value_dot = jnp.einsum("hgqd,khd->hgqk", accum_grad, value_grid, preferred_element_type=f32)
        score_grad = (weights * (value_dot - row_term[..., None])).astype(bf16)
        query_part = (
            jnp.einsum("hgqk,khd->hgqd", score_grad, key_grid, preferred_element_type=f32)
            * score_scale
        )
        key_part = (
            jnp.einsum("hgqk,hgqd->khd", score_grad, query_seq, preferred_element_type=f32)
            * score_scale
        )
        value_part = jnp.einsum(
            "hgqk,hgqd->khd", weights.astype(bf16), accum_grad, preferred_element_type=f32
        )
        return (
            query_part,
            key_part.reshape(full_rows, kv_heads * HEAD_DIMENSION),
            value_part.reshape(full_rows, kv_heads * HEAD_DIMENSION),
        )

    query_grads, key_grads, value_grads = lax.map(
        sequence_back,
        (query_vectors, key_again, value_again, row_max, row_total, attention_out, head_grad),
    )
    key_shards, value_shards = (
        lax.psum_scatter(
            key_grads.astype(jnp.bfloat16), CX, scatter_dimension=1, tiled=True
        ).astype(jnp.float32),
        lax.psum_scatter(
            value_grads.astype(jnp.bfloat16), CX, scatter_dimension=1, tiled=True
        ).astype(jnp.float32),
    )
    query_back = (
        rotate_back(
            query_grads.transpose(0, 3, 1, 2, 4).reshape(
                sequence_count, sequence_rows, local_heads, HEAD_DIMENSION
            ),
            cosine,
            sine_part,
        )
        .reshape(token_count, local_heads * HEAD_DIMENSION)
        .astype(bf16)
    )
    key_back = (
        rotate_back(
            key_shards.reshape(sequence_count, sequence_rows, kv_heads, HEAD_DIMENSION),
            cosine,
            sine_part,
        )
        .reshape(token_count, kv_heads * HEAD_DIMENSION)
        .astype(bf16)
    )
    value_back = value_shards.reshape(token_count, kv_heads * HEAD_DIMENSION).astype(bf16)
    query_wgrad = contract_rows(first_normalized, query_back)
    key_wgrad = contract_rows(first_normalized, key_back)
    value_wgrad = contract_rows(first_normalized, value_back)
    normed_one_part = (
        contract_cols(query_back, query_matrix)
        + contract_cols(key_back, projected_keys)
        + contract_cols(value_back, projected_values)
    )
    normed_one_grad, forward_gain_sum = (
        lax.psum(normed_one_part.astype(jnp.bfloat16), TP).astype(jnp.float32),
        lax.psum(forward_gain_part.astype(jnp.bfloat16), TP).astype(jnp.float32),
    )
    mixer_back, mixer_gain_part = norm_back(stream_in, inverse_one, mixer_scale, normed_one_grad)
    input_field = (stream_grad + mixer_back).reshape(sequence_count, sequence_rows, model_width)
    shards = (
        lax.psum_scatter(
            query_wgrad.astype(jnp.bfloat16), (DP, CX), scatter_dimension=0, tiled=True
        ).astype(jnp.float32),
        lax.psum_scatter(
            key_wgrad.astype(jnp.bfloat16), (DP, CX), scatter_dimension=0, tiled=True
        ).astype(jnp.float32),
        lax.psum_scatter(
            value_wgrad.astype(jnp.bfloat16), (DP, CX), scatter_dimension=0, tiled=True
        ).astype(jnp.float32),
        lax.psum_scatter(
            output_grad.astype(jnp.bfloat16), (DP, CX), scatter_dimension=1, tiled=True
        ).astype(jnp.float32),
        lax.psum_scatter(
            gate_grad.astype(jnp.bfloat16), (DP, CX), scatter_dimension=0, tiled=True
        ).astype(jnp.float32),
        lax.psum_scatter(
            up_grad.astype(jnp.bfloat16), (DP, CX), scatter_dimension=0, tiled=True
        ).astype(jnp.float32),
        lax.psum_scatter(
            down_grad.astype(jnp.bfloat16), (DP, CX), scatter_dimension=1, tiled=True
        ).astype(jnp.float32),
        lax.psum_scatter(
            mixer_gain_part.astype(jnp.bfloat16), (DP, CX), scatter_dimension=0, tiled=True
        ).astype(jnp.float32),
        lax.psum_scatter(
            forward_gain_sum.astype(jnp.bfloat16),
            (DP, CX),
            scatter_dimension=0,
            tiled=True,
        ).astype(jnp.float32),
    )
    masters = (
        query_weight,
        key_weight,
        value_projection,
        output_weight,
        gate_weight,
        up_weight,
        down_weight,
        attention_gain,
        feedforward_gain,
    )
    moments_one = (
        query_weight_first,
        key_projection_first_moment,
        value_projection_first_moment,
        output_weight_first,
        gate_weight_first,
        up_weight_first,
        down_weight_first,
        attention_gain_first,
        feedforward_gain_first,
    )
    moments_two = (
        query_weight_second,
        key_projection_second_moment,
        value_projection_second_moment,
        output_weight_second,
        gate_weight_second,
        up_weight_second,
        down_weight_second,
        attention_gain_second,
        feedforward_gain_second,
    )
    matrix_rate = 1.0 / math.sqrt(MODEL_DIMENSION)
    output_rate = 1.0 / math.sqrt(8 * QUERY_HEADS * HEAD_DIMENSION // full_rows)
    rates = (matrix_rate,) * 3 + (output_rate,) + (matrix_rate,) * 3 + (gain_rate,) * 2
    decays = (decay_rate,) * 7 + (0.0,) * 2
    updates = [
        adamw_update(weight, gradient, moment_one, moment_two, rate_value, decay_value)
        for weight, gradient, moment_one, moment_two, rate_value, decay_value in zip(
            masters, shards, moments_one, moments_two, rates, decays
        )
    ]
    return (
        output_field,
        input_field,
        shards[0],
        shards[1],
        shards[2],
        shards[3],
        shards[4],
        shards[5],
        shards[6],
        shards[7],
        shards[8],
        updates[0][0],
        updates[1][0],
        updates[2][0],
        updates[3][0],
        updates[4][0],
        updates[5][0],
        updates[6][0],
        updates[7][0],
        updates[8][0],
        updates[0][1],
        updates[1][1],
        updates[2][1],
        updates[3][1],
        updates[4][1],
        updates[5][1],
        updates[6][1],
        updates[7][1],
        updates[8][1],
        updates[0][2],
        updates[1][2],
        updates[2][2],
        updates[3][2],
        updates[4][2],
        updates[5][2],
        updates[6][2],
        updates[7][2],
        updates[8][2],
    )


def hidden_kernel(tile, normed, upstream, both_w, down_w, hidden, dboth, dnormed, acc):
    gate_up = nn(normed[...], both_w[...]).astype(bf16).astype(f32)
    gate, up = gate_up[:, :tile], gate_up[:, tile:]
    sigmoid = 1.0 / (1.0 + jnp.exp(-gate))
    silu = gate * sigmoid
    hidden[...] = (silu * up).astype(bf16)
    dhidden = nn(upstream[...], down_w[...])
    dgate = dhidden * up * sigmoid * (1.0 + gate * (1.0 - sigmoid))
    dboth_low = jnp.concatenate([dgate.astype(bf16), (dhidden * silu).astype(bf16)], axis=1)
    dboth[...] = dboth_low
    step = nt(dboth_low, both_w[...])

    @pl.when(pl.program_id(0) == 0)
    def _():
        acc[...] = step

    @pl.when(pl.program_id(0) > 0)
    def _():
        acc[...] += step

    @pl.when(pl.program_id(0) == pl.num_programs(0) - 1)
    def _():
        dnormed[...] = acc[...].astype(bf16)


def feed_forward(normed, upstream, weights, ff):
    rows, model = normed.shape
    tile = FF_TILE
    tiles = ff // tile
    whole = pl.BlockSpec((rows, model), lambda j: (0, 0))
    return pl.pallas_call(
        functools.partial(hidden_kernel, tile),
        grid=(tiles,),
        in_specs=[
            whole,
            whole,
            pl.BlockSpec((model, 2 * tile), lambda j: (0, j)),
            pl.BlockSpec((model, tile), lambda j: (0, 2 * tiles + j)),
        ],
        out_specs=[
            pl.BlockSpec((rows, tile), lambda j: (0, j)),
            pl.BlockSpec((rows, 2 * tile), lambda j: (0, j)),
            whole,
        ],
        out_shape=[
            jax.ShapeDtypeStruct((rows, ff), bf16),
            jax.ShapeDtypeStruct((rows, 2 * ff), bf16),
            jax.ShapeDtypeStruct((rows, model), bf16),
        ],
        scratch_shapes=[pltpu.VMEM((rows, model), f32)],
        compiler_params=pltpu.CompilerParams(vmem_limit_bytes=56 * 1024 * 1024),
        cost_estimate=LARGE,
        name="feed_forward",
    )(normed, upstream, weights, weights)


def mix_kernel(x, own, other, gain, w_own, w_other, stream, normed):
    total = x[...].astype(f32) + nt(own[...], w_own[...]) + nt(other[...], w_other[...])
    stream[...] = total
    inverse = lax.rsqrt(jnp.mean(total * total, axis=-1, keepdims=True) + norm_eps)
    normed[...] = (total * inverse * gain[...]).astype(bf16)


def mix_heads(x, own, other, gain, weights, first_col):
    rows, model = x.shape
    width = own.shape[1]
    tile = 256
    at = first_col // width
    row_block = lambda cols: pl.BlockSpec((tile, cols), lambda r: (r, 0))
    return pl.pallas_call(
        mix_kernel,
        grid=(rows // tile,),
        in_specs=[
            row_block(model),
            row_block(width),
            row_block(width),
            pl.BlockSpec((1, model), lambda r: (0, 0)),
            pl.BlockSpec((model, width), lambda r: (0, at)),
            pl.BlockSpec((model, width), lambda r: (0, at + 1)),
        ],
        out_specs=[row_block(model), row_block(model)],
        out_shape=[
            jax.ShapeDtypeStruct((rows, model), f32),
            jax.ShapeDtypeStruct((rows, model), bf16),
        ],
        compiler_params=pltpu.CompilerParams(vmem_limit_bytes=48 * 1024 * 1024),
        cost_estimate=SMALL,
        name="mix_heads",
    )(x, own, other, gain, weights, weights)


def stream_back_kernel(stream, upstream, own, other, gain, w, dstream, dlow, dheads):
    values = stream[...]
    inverse = lax.rsqrt(jnp.mean(values * values, axis=-1, keepdims=True) + norm_eps)
    unit = values * inverse
    scaled = gain[...] * (own[...].astype(f32) + other[...].astype(f32))
    back = inverse * (scaled - unit * jnp.mean(scaled * unit, axis=-1, keepdims=True))
    total = upstream[...].astype(f32) + back
    dstream[...] = total
    low = total.astype(bf16)
    dlow[...] = low
    dheads[...] = nn(low, w[...]).astype(bf16).T


def stream_back(other, stream, upstream, own, gain, weights, first_col, width):
    rows, model = stream.shape
    tile = 256
    at = first_col // width
    row_block = pl.BlockSpec((tile, model), lambda r: (r, 0))
    return pl.pallas_call(
        stream_back_kernel,
        grid=(rows // tile,),
        in_specs=[row_block] * 4
        + [pl.BlockSpec((1, model), lambda r: (0, 0)), pl.BlockSpec((model, width), lambda r: (0, at))],
        out_specs=[row_block, row_block, pl.BlockSpec((width, tile), lambda r: (0, r))],
        out_shape=[
            jax.ShapeDtypeStruct((rows, model), f32),
            jax.ShapeDtypeStruct((rows, model), bf16),
            jax.ShapeDtypeStruct((width, rows), bf16),
        ],
        compiler_params=pltpu.CompilerParams(vmem_limit_bytes=48 * 1024 * 1024),
        cost_estimate=LARGE,
        name="stream_back",
    )(stream, upstream, own, other, gain, weights)


def gradient_kernel(count, order, *refs):
    left, right = refs[:2 * count], refs[2 * count:3 * count]
    kept, sent = refs[3 * count:]
    total = 0.0
    for s in range(count):
        rows = jnp.concatenate([left[2 * s][...], left[2 * s + 1][...]], axis=1)
        total = total + lax.dot_general(
            rows, right[s][...], (((0,), (0,)), ((), ())), preferred_element_type=f32
        )
    low = total.astype(bf16)

    @pl.when(pl.program_id(0) == 0)
    def _():
        kept[...] = low

    @pl.when(pl.program_id(0) == 1)
    def _():
        sent[...] = low


def gradient(left, right, order, tile):
    rows, model = left[0].shape
    cols = right[0].shape[1]
    quarter = model // 4
    tiles = cols // tile
    count = len(left)
    left_specs = [
        pl.BlockSpec((rows, quarter), functools.partial(lambda p, h, c, order: (0, order[2 * h + p]), p))
        for p in range(2)
    ]
    return pl.pallas_call(
        functools.partial(gradient_kernel, count),
        grid_spec=pltpu.PrefetchScalarGridSpec(
            num_scalar_prefetch=1,
            grid=(2, tiles),
            in_specs=left_specs * count
            + [pl.BlockSpec((rows, tile), lambda h, c, order: (0, c))] * count,
            out_specs=[
                pl.BlockSpec((2 * quarter, tile), lambda h, c, order: (0, jnp.where(h == 0, c, tiles - 1))),
                pl.BlockSpec((2 * quarter, tile), lambda h, c, order: (0, jnp.where(h == 0, 0, c))),
            ],
        ),
        out_shape=[jax.ShapeDtypeStruct((2 * quarter, cols), bf16)] * 2,
        compiler_params=pltpu.CompilerParams(vmem_limit_bytes=56 * 1024 * 1024),
        cost_estimate=LARGE,
        name="gradient",
    )(order, *[each for part in left for each in (part, part)], *right)


def feed_kernel(hidden, w, out):
    out[...] = nt(hidden[...], w[...]).astype(bf16)


def feed_out(hidden, weights, first_col):
    rows, ff = hidden.shape
    model = weights.shape[0]
    tile = 512
    return pl.pallas_call(
        feed_kernel,
        grid=(model // tile,),
        in_specs=[
            pl.BlockSpec((rows, ff), lambda c: (0, 0)),
            pl.BlockSpec((tile, ff), lambda c: (c, first_col // ff)),
        ],
        out_specs=pl.BlockSpec((rows, tile), lambda c: (0, c)),
        out_shape=jax.ShapeDtypeStruct((rows, model), bf16),
        compiler_params=pltpu.CompilerParams(vmem_limit_bytes=48 * 1024 * 1024),
        cost_estimate=LARGE,
        name="feed_out",
    )(hidden, weights)


def input_back_kernel(q_width, kv_width, odd, dq, kept, first, second, last, cos_t, sin_t, w, dkv, dnormed):
    near = jnp.where(odd[0] == 0, first[0].astype(f32), second[0].astype(f32))
    total = kept[0].astype(f32) + near + last[...].astype(f32)
    cos_part, sin_part = cos_t[...], sin_t[...]
    parts = []
    for h in range(kv_width // HD):
        lead = total[h * HD:h * HD + HALF]
        trail = total[h * HD + HALF:(h + 1) * HD]
        parts += [
            (lead * cos_part + trail * sin_part).astype(bf16),
            (trail * cos_part - lead * sin_part).astype(bf16),
        ]
    parts.append(total[kv_width:].astype(bf16))
    rows = jnp.concatenate(parts, axis=0).T
    dkv[...] = rows
    low = nt(dq[...], w[:, :q_width]) + nt(rows, w[:, q_width:q_width + 2 * kv_width])
    dnormed[...] = low.astype(bf16)


def input_back(dq, odd, kept, arrived, last, cos_t, sin_t, weights):
    rows, q_width = dq.shape
    kv_width = kept.shape[1] // 2
    model = weights.shape[0]
    tile = 256
    table = pl.BlockSpec((HALF, tile), lambda r: (0, r))
    piece = lambda at: pl.BlockSpec((1, 2 * kv_width, tile), lambda r: (at, 0, r))
    return pl.pallas_call(
        functools.partial(input_back_kernel, q_width, kv_width),
        grid=(rows // tile,),
        in_specs=[
            pl.BlockSpec(memory_space=pltpu.SMEM),
            pl.BlockSpec((tile, q_width), lambda r: (r, 0)),
            piece(0),
            piece(0),
            piece(1),
            pl.BlockSpec((2 * kv_width, tile), lambda r: (0, r)),
            table,
            table,
            pl.BlockSpec(weights.shape, lambda r: (0, 0)),
        ],
        out_specs=[
            pl.BlockSpec((tile, 2 * kv_width), lambda r: (r, 0)),
            pl.BlockSpec((tile, model), lambda r: (r, 0)),
        ],
        out_shape=[
            jax.ShapeDtypeStruct((rows, 2 * kv_width), bf16),
            jax.ShapeDtypeStruct((rows, model), bf16),
        ],
        compiler_params=pltpu.CompilerParams(vmem_limit_bytes=48 * 1024 * 1024),
        cost_estimate=LARGE,
        name="input_back",
    )(odd, dq, kept, arrived, arrived, last, cos_t, sin_t, weights)


def output_kernel(stream, feed, other, before, out):
    out[0] = stream[...] + feed[...].astype(f32) + other[...].astype(f32)


def finish_output(other, stream, feed, part, parts, before):
    rows, model = stream.shape
    tile = 256
    block = pl.BlockSpec((tile, model), lambda r: (r, 0))
    return pl.pallas_call(
        output_kernel,
        grid=(rows // tile,),
        in_specs=[block, block, block, pl.BlockSpec(memory_space=pl.ANY)],
        out_specs=pl.BlockSpec((1, tile, model), lambda r: (part, r, 0)),
        out_shape=jax.ShapeDtypeStruct((parts, rows, model), f32),
        input_output_aliases={3: 0} if before.ndim == 3 else {},
        compiler_params=pltpu.CompilerParams(vmem_limit_bytes=32 * 1024 * 1024),
        cost_estimate=LARGE,
        name="finish_output",
    )(stream, feed, other, before)


def input_kernel(dstream, x, own, other, gain, before, out):
    values = x[...].astype(f32)
    inverse = lax.rsqrt(jnp.mean(values * values, axis=-1, keepdims=True) + norm_eps)
    unit = values * inverse
    scaled = gain[...] * (own[...].astype(f32) + other[...].astype(f32))
    back = inverse * (scaled - unit * jnp.mean(scaled * unit, axis=-1, keepdims=True))
    out[0] = dstream[...] + back


def finish_input(other, dstream, x, own, gain, part, parts, before):
    rows, model = dstream.shape
    tile = 256
    block = pl.BlockSpec((tile, model), lambda r: (r, 0))
    return pl.pallas_call(
        input_kernel,
        grid=(rows // tile,),
        in_specs=[block] * 4
        + [pl.BlockSpec((1, model), lambda r: (0, 0)), pl.BlockSpec(memory_space=pl.ANY)],
        out_specs=pl.BlockSpec((1, tile, model), lambda r: (part, r, 0)),
        out_shape=jax.ShapeDtypeStruct((parts, rows, model), f32),
        input_output_aliases={5: 0} if before.ndim == 3 else {},
        compiler_params=pltpu.CompilerParams(vmem_limit_bytes=32 * 1024 * 1024),
        cost_estimate=LARGE,
        name="finish_input",
    )(dstream, x, own, other, gain, before)


def interleave(gate, up):
    rows, ff = gate.shape
    pair = jnp.stack([gate.reshape(rows, -1, FF_TILE), up.reshape(rows, -1, FF_TILE)], axis=2)
    return pair.reshape(rows, 2 * ff)


def exchange(values, axis, step):
    size = lax.axis_size(axis)
    return lax.ppermute(values, axis, [(i, i ^ step) for i in range(size)])


def swap(values):
    return exchange(values, TP, 1)


def ring_blocks(block):
    size = lax.axis_size(CX)
    blocks = [block]
    for _ in range(size - 1):
        blocks.append(lax.ppermute(blocks[-1], CX, [(i, (i + 1) % size) for i in range(size)]))
    return blocks


def add_low(a, b):
    return (a.astype(f32) + b.astype(f32)).astype(bf16)


def after(value, *earlier):
    return lax.optimization_barrier((value,) + earlier)[0]


class Line:
    def __init__(self):
        self.last = ()

    def put(self, function, first, *rest):
        first = lax.optimization_barrier((first,) + self.last)[0]
        result = function(first, *rest)
        self.last = (jax.tree.leaves(result)[0],)
        return result


def core_add(kept, arrived):
    half = kept.shape[0] // 2
    return add_low(kept[half:], arrived[half:]), add_low(kept[:half], arrived[:half])


def copy_kernel(source, out):
    out[...] = source[...]


def copy_out(values):
    return pl.pallas_call(
        copy_kernel,
        out_shape=jax.ShapeDtypeStruct(values.shape, values.dtype),
        cost_estimate=LARGE,
        name="copy_out",
    )(values)


def near_pick(held, low):
    grid = held.reshape(2, 2, held.shape[0] // 4, held.shape[1])
    return lax.dynamic_index_in_dim(grid, low, axis=1, keepdims=False)


def far_pick(pair, high):
    return lax.dynamic_index_in_dim(pair, high, axis=0, keepdims=False)


def line_add(held, arrived):
    total = add_low(held, arrived)
    low = lax.axis_index(CX) % 2
    return near_pick(total, 1 - low), near_pick(total, low)


def near_add(held, arrived):
    total = add_low(held, arrived)
    high = lax.axis_index(CX) // 2
    return far_pick(total, 1 - high), far_pick(total, high)


def far_add(held, arrived):
    return held.astype(f32) + arrived.astype(f32)


def far_part(kept, arrived, odd):
    return add_low(kept[1], jnp.where(odd[0] == 0, arrived[1], arrived[0]))


def join(left, right):
    return tuple(jnp.concatenate(each, axis=1) for each in zip(left, right))


def body(
    tokens, out_grad, span_order,
    query_weight, key_weight, value_projection, output_weight, gate_weight, up_weight, down_weight,
    attention_gain, feedforward_gain, *moments,
):
    moments_one, moments_two = moments[:9], moments[9:]
    shards_axes = (DP, CX)
    sequence_count, sequence_rows, model = tokens.shape
    q_width, kv_width = query_weight.shape[1], key_weight.shape[1]
    ff = gate_weight.shape[1]
    context_size = lax.axis_size(CX)
    span_rows = sequence_rows // 2
    gains_low = jnp.stack([attention_gain, feedforward_gain], axis=1).astype(bf16)

    first_shard = jnp.concatenate(
        [
            query_weight.astype(bf16),
            key_weight.astype(bf16),
            value_projection.astype(bf16),
            jnp.pad(gains_low, ((0, 0), (0, 126))),
        ],
        axis=1,
    )
    head_w = lax.all_gather(first_shard, shards_axes, axis=0, tiled=True)
    out_shard = output_weight.astype(bf16).T
    out_w = lax.all_gather(
        after(jnp.concatenate([out_shard, swap(out_shard)], axis=1), head_w), shards_axes, axis=0, tiled=True
    )
    second_shard = jnp.concatenate(
        [interleave(gate_weight.astype(bf16), up_weight.astype(bf16)), down_weight.astype(bf16).T],
        axis=1,
    )
    gains = head_w[:, q_width + 2 * kv_width:q_width + 2 * kv_width + 2].astype(f32).T
    mixer_scale, forward_scale = gains[0:1], gains[1:2]

    context_index = lax.axis_index(CX)
    ring_slots = jnp.stack(
        [2 * ((context_index - s) % context_size) + t for s in range(context_size) for t in range(2)]
    )
    ring_spans = span_order[ring_slots]
    spans = jnp.concatenate([ring_spans[:2], ring_spans]).astype(jnp.int32)
    positions = (
        spans[:2, None] * span_rows + jnp.arange(span_rows, dtype=jnp.int32)[None, :]
    ).reshape(sequence_rows)
    frequency = rope_base ** (-(jnp.arange(HALF, dtype=f32) * 2.0) / HEAD_DIMENSION)
    angles = frequency[:, None] * positions.astype(f32)[None, :]
    cos_t, sin_t = jnp.cos(angles), jnp.sin(angles)
    odd = (context_index % 2).astype(jnp.int32).reshape(1)
    device = lax.axis_index(DP)
    core, line = device % 2, device // 2
    order = jnp.stack(
        [line * 2 + core, (1 - line) * 2 + core, line * 2 + 1 - core, (1 - line) * 2 + 1 - core]
    ).astype(jnp.int32)

    sequences = range(sequence_count)
    normed_one, queries, blocks = [], [], []
    for s in sequences:
        n1, qt, kv = project(tokens[s], mixer_scale, head_w, cos_t, sin_t, q_width, kv_width)
        normed_one.append(n1)
        queries.append(qt)
        blocks.append(ring_blocks(kv))
    rest_w = lax.all_gather(
        after(second_shard, *[each[0] for each in blocks]), shards_axes, axis=0, tiled=True
    )
    attended = [attention_forward(spans, queries[s], blocks[s]) for s in sequences]
    streams, normed_two = [], []
    for s in sequences:
        own = attended[s][0]
        stream, n2 = mix_heads(tokens[s], own, swap(own), forward_scale, out_w, 0)
        streams.append(stream)
        normed_two.append(n2)
    line = Line()
    hiddens, dboths, dnormed, others = [], [], [], []
    for s in sequences:
        hidden, dboth, dn2 = line.put(feed_forward, normed_two[s], out_grad[s], rest_w, ff)
        hiddens.append(hidden)
        dboths.append(dboth)
        dnormed.append(dn2)
        others.append(swap(line.put(copy_out, dn2)))

    def back(s):
        return line.put(
            stream_back, others[s], streams[s], out_grad[s], dnormed[s], forward_scale, out_w, 0, q_width
        )

    def attend_back(s, dheads):
        return line.put(
            attention_backward, dheads, spans, queries[s], attended[s][1], attended[s][2], cos_t, sin_t, blocks[s]
        )

    grads = lambda left, right, tile: line.put(gradient, left, right, order, tile)
    masters = (
        query_weight, key_weight, value_projection, output_weight, gate_weight, up_weight, down_weight,
        attention_gain, feedforward_gain,
    )
    full_rows = span_order.shape[0] * span_rows
    matrix_rate = 1.0 / math.sqrt(MODEL_DIMENSION)
    output_rate = 1.0 / math.sqrt(8 * QUERY_HEADS * HEAD_DIMENSION // full_rows)
    rates = (matrix_rate,) * 3 + (output_rate,) + (matrix_rate,) * 3 + (gain_rate,) * 2
    decays = (decay_rate,) * 7 + (0.0,) * 2

    def update(at, shard):
        return (shard,) + adamw_update(
            masters[at], shard, moments_one[at], moments_two[at], rates[at], decays[at]
        )

    def finish_down(mine, far):
        return (update(6, far_add(mine, far).T),)

    def finish_both(mine, far):
        total = far_add(mine, far)
        pair = total.reshape(total.shape[0], -1, 2, FF_TILE)
        sums = jnp.sum(total * second_shard[:, :2 * ff].astype(f32), axis=1)
        return update(4, pair[:, :, 0].reshape(-1, ff)), update(5, pair[:, :, 1].reshape(-1, ff)), sums

    def finish_mid(mine, far):
        total = far_add(mine, far)
        query = total[:, q_width:]
        sums = jnp.sum(query * first_shard[:, :q_width].astype(f32), axis=1)
        return update(0, query), update(3, total[:, :q_width].T), sums

    def finish_kv(mine, far):
        total = far_add(mine, far)
        sums = jnp.sum(total * first_shard[:, q_width:q_width + 2 * kv_width].astype(f32), axis=1)
        return update(1, total[:, :kv_width]), update(2, total[:, kv_width:]), sums

    down_kept, down_sent = grads([out_grad[s] for s in sequences], hiddens, GRAD_TILE)
    down_core = exchange(down_sent, DP, 1)
    dstream_a, dlow_a, dheads_a = back(0)
    down_passed, down_held = line.put(core_add, down_kept, down_core)
    down_line = exchange(down_passed, DP, 2)
    dq_a, kept_a, sent_a = attend_back(0, dheads_a)
    arrived_a = exchange(line.put(copy_out, sent_a), CX, 1)
    both_kept, both_sent = grads(normed_two, dboths, GRAD_TILE)
    both_core = exchange(both_sent, DP, 1)
    dstream_b, dlow_b, dheads_b = back(1)
    both_passed, both_held = line.put(core_add, both_kept, both_core)
    both_line = exchange(both_passed, DP, 2)
    last_a = exchange(line.put(far_part, kept_a, arrived_a, odd), CX, 2)
    down_away, down_mine = line.put(line_add, down_held, down_line)
    down_near = exchange(down_away, CX, 1)
    dq_b, kept_b, sent_b = attend_back(1, dheads_b)
    arrived_b = exchange(line.put(copy_out, sent_b), CX, 1)
    feed_a = line.put(feed_out, hiddens[0], rest_w, 2 * ff)
    feed_other_a = swap(feed_a)
    down_away, down_mine = line.put(near_add, down_mine, down_near)
    down_far = exchange(down_away, CX, 2)
    dkv_a, dn1_a = line.put(input_back, dq_a, odd, kept_a, arrived_a, last_a, cos_t, sin_t, head_w)
    dn1_other_a = swap(line.put(copy_out, dn1_a))
    output_parts = grads([dlow_a, dlow_b], [each[0] for each in attended], q_width)
    query_parts = grads(normed_one, [dq_a, dq_b], q_width)
    mid_kept, mid_sent = line.put(join, output_parts, query_parts)
    mid_core = exchange(mid_sent, DP, 1)
    last_b = exchange(line.put(far_part, kept_b, arrived_b, odd), CX, 2)
    output_field = line.put(finish_output, feed_other_a, streams[0], feed_a, 0, sequence_count, order)
    mid_passed, mid_held = line.put(core_add, mid_kept, mid_core)
    mid_line = exchange(mid_passed, DP, 2)
    (down_done,) = line.put(finish_down, down_mine, down_far)
    both_away, both_mine = line.put(line_add, both_held, both_line)
    both_near = exchange(both_away, CX, 1)
    dkv_b, dn1_b = line.put(input_back, dq_b, odd, kept_b, arrived_b, last_b, cos_t, sin_t, head_w)
    kv_kept, kv_sent = grads(normed_one, [dkv_a, dkv_b], 2 * kv_width)
    kv_core = exchange(kv_sent, DP, 1)
    dn1_other_b = swap(line.put(copy_out, dn1_b))
    input_field = line.put(
        finish_input, dn1_other_a, dstream_a, tokens[0], dn1_a, mixer_scale, 0, sequence_count, order
    )
    kv_passed, kv_held = line.put(core_add, kv_kept, kv_core)
    kv_line = exchange(kv_passed, DP, 2)
    both_away, both_mine = line.put(near_add, both_mine, both_near)
    both_far = exchange(both_away, CX, 2)
    mid_away, mid_mine = line.put(line_add, mid_held, mid_line)
    mid_near = exchange(mid_away, CX, 1)
    feed_b = line.put(feed_out, hiddens[1], rest_w, 2 * ff)
    feed_other_b = swap(feed_b)
    kv_away, kv_mine = line.put(line_add, kv_held, kv_line)
    kv_near = exchange(kv_away, CX, 1)
    mid_away, mid_mine = line.put(near_add, mid_mine, mid_near)
    mid_far = exchange(mid_away, CX, 2)
    input_field = line.put(
        finish_input, dn1_other_b, dstream_b, tokens[1], dn1_b, mixer_scale, 1, sequence_count, input_field
    )
    kv_away, kv_mine = line.put(near_add, kv_mine, kv_near)
    kv_far = exchange(kv_away, CX, 2)
    gate_done, up_done, both_sums = line.put(finish_both, both_mine, both_far)
    query_done, output_done, query_sums = line.put(finish_mid, mid_mine, mid_far)
    output_field = line.put(
        finish_output, feed_other_b, streams[1], feed_b, 1, sequence_count, output_field
    )
    key_done, value_done, kv_sums = line.put(finish_kv, kv_mine, kv_far)
    row_sums = jnp.stack([query_sums + kv_sums, both_sums])
    gain_shard = (row_sums + swap(row_sums)) / gains_low.astype(f32).T
    done = (
        query_done, key_done, value_done, output_done, gate_done, up_done, down_done,
        update(7, gain_shard[0]), update(8, gain_shard[1]),
    )
    return (output_field, input_field) + tuple(each[part] for part in range(4) for each in done)


def solution(mesh):
    rows, cols, gains = P((DP, CX), TP), P(TP, (DP, CX)), P((DP, CX))
    stream = P(DP, CX, None)
    params = (rows,) * 3 + (cols,) + (rows,) * 2 + (cols,) + (gains,) * 2
    fast = (
        mesh.shape[TP] == 2
        and mesh.shape[DP] == 4
        and mesh.shape[CX] == 4
        and (KEY_VALUE_HEADS // 2 * HEAD_DIMENSION) % 128 == 0
    )
    return jax.shard_map(
        body if fast else plain_body,
        mesh=mesh,
        in_specs=(stream, stream, P()) + params * 3,
        out_specs=(stream, stream) + params * 4,
        check_vma=False,
    )
```
